32 devices in a mesh: slab: 8 (over y, x, core), chan: 4 (over z).
Axes of the slice: x: 2, y: 2, z: 4, core: 2. Of those that a mesh axis runs over, the one named last changes fastest.
Arguments:
- inputs: bfloat16 [256, 16, 1536], P('chan', 'slab'), may hold values from -6 to 6
- filters: bfloat16 [27, 256, 256], P(None, 'chan'), may hold values from -0.078125 to 0.078125
- cotangent: bfloat16 [256, 16, 1536], P('chan', 'slab'), may hold values from -6 to 6
Outputs:
- features: bfloat16 [256, 16, 1536], P('chan', 'slab')
- input_grad: bfloat16 [256, 16, 1536], P('chan', 'slab')
- filter_grad: float32 [27, 256, 256], P(None, 'chan', 'slab')
The draws below stay inside these ranges and needn't reach their ends.
All inputs are finite; a program needn't handle non-finite values.
Results may differ from the reference program's by a relative error of at most 0.001.
Values may be sent and summed in bfloat16 or wider, within the bound.
A program may use at most 128 MiB of HBM per device.

```python
import math
import jax
import jax.numpy as jnp

CIN = 256
COUT = 256
H = 24
W = 64
DEPTH = 16
HW = 1536


def with_spikes(entries, own_key, source, target, blocks, factor):
    def block_of(axis_at):
        return (jnp.arange(entries.shape[axis_at]) // (entries.shape[axis_at] // blocks)).reshape((-1,) + (1,) * (entries.ndim - 1 - axis_at))

    one_side = jax.random.permutation(own_key, blocks)[block_of(target)]
    other_side = (block_of(target) + blocks // 2) % blocks
    return jnp.where((block_of(source) == one_side) | (block_of(source) == other_side), factor * entries, entries)


def block_levels(rng, shape, cuts, smallest, high):
    def one(position, blocks):
        steps = jax.random.uniform(jax.random.fold_in(jax.random.fold_in(rng, 6), position), (blocks,), jnp.float32, smallest / len(cuts), high / len(cuts))
        return jnp.repeat(jnp.exp(steps), shape[position] // blocks).reshape((-1,) + (1,) * (len(shape) - position - 1))

    level = one(*cuts[0])
    for cut in cuts[1:]:
        level = level * one(*cut)
    return level


def bell_draw(stream_key, extent, scale, bound, cuts=(), kind=jnp.bfloat16):
    result = scale * jax.random.normal(stream_key, extent, jnp.float32)
    if cuts:
        result = result * block_levels(stream_key, extent, cuts, -0.22, 0.18)
    return jnp.clip(result, -bound, bound).astype(kind)


def gaussian_with(key, dims, deviation, bound, split, heavy, held_as=jnp.bfloat16):
    values = deviation * jax.random.normal(key, dims, jnp.float32)
    if split:
        values = values * block_levels(key, dims, split, -0.22, 0.18)
    return jnp.clip(with_spikes(values, jax.random.fold_in(key, 3), *heavy), -bound, bound).astype(held_as)


def setup_inputs(seed: int = 0) -> dict:
    key_list = jax.random.split(jax.random.key(seed), 4)
    return {
        "inputs": gaussian_with(key_list[0], (CIN, DEPTH, HW), 1.0, 6.0, ((0, 4), (1, 8)), (1, 0, 8, 2.0)),
        "filters": bell_draw(key_list[1], (27, COUT, CIN), (27 * CIN) ** -0.5, 0.078125, ((1, 4),)),
        "cotangent": bell_draw(key_list[2], (COUT, DEPTH, HW), 1.0, 6.0, ((0, 4), (1, 8))),
    }


offsets = (-1, 0, 1)

def reference(inputs, filters, cotangent):
    cells = DEPTH * H * W
    volume = inputs.reshape(CIN, DEPTH, H, W)
    grad_volume = cotangent.reshape(COUT, DEPTH, H, W)
    grad_flat = cotangent.reshape(COUT, cells)
    factor = 1.0 / math.sqrt(cells)
    features = jnp.zeros((COUT, cells), jnp.float32)
    input_grad = jnp.zeros((CIN, cells), jnp.float32)
    blocks = []
    for plane_shift in offsets:
        for row_shift in offsets:
            for column_shift in offsets:
                tap_index = 9 * (plane_shift + 1) + 3 * (row_shift + 1) + column_shift + 1
                shifted = jnp.roll(volume, (-plane_shift, -row_shift, -column_shift), axis=(1, 2, 3)).reshape(CIN, cells)
                unshifted = jnp.roll(grad_volume, (plane_shift, row_shift, column_shift), axis=(1, 2, 3)).reshape(COUT, cells)
                features = features + jnp.dot(filters[tap_index], shifted, preferred_element_type=jnp.float32)
                input_grad = input_grad + jnp.dot(filters[tap_index].T, unshifted, preferred_element_type=jnp.float32)
                blocks.append(jnp.dot(grad_flat, shifted.T, preferred_element_type=jnp.float32) * factor)
    features = features.astype(jnp.bfloat16).reshape(COUT, DEPTH, H * W)
    input_grad = input_grad.astype(jnp.bfloat16).reshape(CIN, DEPTH, H * W)
    return (features, input_grad, jnp.stack(blocks))
```

```python
import functools
import math

import jax
import jax.numpy as jnp
from jax import lax
from jax.experimental import pallas as pl
from jax.experimental.pallas import tpu as pltpu
from jax.sharding import PartitionSpec as P

W = 64
MESH = pl.DeviceIdType.MESH
F32 = jnp.float32
BF16 = jnp.bfloat16


def turn_and_shift(src, dst):
    planes, channels, cells = src.shape
    for s in range(planes):

        def step(m, carry):
            turned = src[s, :, pl.ds(pl.multiple_of(m * 128, 128), 128)].astype(F32).T
            for h in range(128 // W):
                row = turned[h * W : (h + 1) * W]
                at = pl.ds(pl.multiple_of(m * 128 + (h + 1) * W, W), W)
                dst[0, s, at, :] = pltpu.roll(row, 1, 0).astype(BF16)
                dst[1, s, at, :] = row.astype(BF16)
                dst[2, s, at, :] = pltpu.roll(row, W - 1, 0).astype(BF16)
            return carry

        lax.fori_loop(0, cells // 128, step, 0)
        for r in range(3):
            dst[r, s, 0:W, :] = dst[r, s, cells : cells + W, :]
            dst[r, s, cells + W : cells + 2 * W, :] = dst[r, s, W : 2 * W, :]


def conv(src, weights, y):
    planes, rows, cells = y.shape
    chunk = 512
    for s in range(planes):

        def step(n, carry):
            total = None
            for q in range(3):
                for r in range(3):
                    part = jnp.dot(
                        src[r, s, pl.ds(pl.multiple_of(n * chunk + q * W, W), chunk), :],
                        weights[3 * q + r],
                        preferred_element_type=F32,
                    )
                    total = part if total is None else total + part
            y[s, :, pl.ds(pl.multiple_of(n * chunk, chunk), chunk)] = total.T
            return carry

        lax.fori_loop(0, cells // chunk, step, 0)


def finish(y, rim, out):
    planes = y.shape[0]
    ch = out.shape[1]
    for d in range(planes):
        total = y[d, ch : 2 * ch, :]
        total = total + (y[d - 1, 0:ch, :] if d > 0 else rim[0])
        total = total + (y[d + 1, 2 * ch : 3 * ch, :] if d < planes - 1 else rim[1])
        out[d] = total.astype(out.dtype)


def kernel(
    S, C, factor,
    x, g, wf, wt,
    feat, igrad, dw,
    xg, gg, wg, xt, gt, yx, yg, g3, grim, xrim, irim, dwt, dwr,
    own_sem, x_s, x_r, g_s, g_r, w_s, w_r, gr_s, gr_r, xr_s, xr_r, ir_s, ir_r, d_s, d_r,
):
    planes, ch, cells = x.shape
    cs = dwt.shape[1] // S
    me_s = lax.axis_index("slab")
    me_c = lax.axis_index("chan")

    barrier = pltpu.get_barrier_semaphore()
    for k in range(1, S):
        pl.semaphore_signal(barrier, inc=1, device_id={"slab": lax.rem(me_s + k, S)}, device_id_type=MESH)
    for k in range(1, C):
        pl.semaphore_signal(barrier, inc=1, device_id={"chan": lax.rem(me_c + k, C)}, device_id_type=MESH)
    pl.semaphore_wait(barrier, S - 1 + C - 1)

    mine = pl.ds(pl.multiple_of(me_c * ch, ch), ch)

    def to_chan(k, src, dst, send, recv):
        return pltpu.make_async_remote_copy(
            src_ref=src, dst_ref=dst, send_sem=send.at[k - 1], recv_sem=recv.at[k - 1],
            device_id={"chan": lax.rem(me_c + k, C)}, device_id_type=MESH,
        )

    def to_slab(k, src, dst, send, recv, slot):
        return pltpu.make_async_remote_copy(
            src_ref=src, dst_ref=dst, send_sem=send.at[slot], recv_sem=recv.at[slot],
            device_id={"slab": lax.rem(me_s + k, S)}, device_id_type=MESH,
        )

    def rims(low, high, dst, send, recv):
        return [
            to_slab(1, high, dst.at[0], send, recv, 0),
            to_slab(S - 1, low, dst.at[1], send, recv, 1),
        ]

    x_copies = [to_chan(k, x, xg.at[:, mine, :], x_s, x_r) for k in range(1, C)]
    for c in x_copies:
        c.start()
    g_rims = rims(g.at[0], g.at[planes - 1], grim, gr_s, gr_r)
    for c in g_rims:
        c.start()
    own = [
        pltpu.make_async_copy(x, xg.at[:, mine, :], own_sem.at[0]),
        pltpu.make_async_copy(g, gg.at[:, mine, :], own_sem.at[1]),
        pltpu.make_async_copy(wt.at[me_c], wg.at[:, mine, :], own_sem.at[2]),
    ]
    for c in own:
        c.start()
    for c in own:
        c.wait()
    for c in x_copies:
        c.wait_send()
    g_copies = [to_chan(k, g, gg.at[:, mine, :], g_s, g_r) for k in range(1, C)]
    w_copies = [
        to_chan(k, wt.at[lax.rem(me_c + k, C)], wg.at[:, mine, :], w_s, w_r) for k in range(1, C)
    ]
    for c in g_copies + w_copies:
        c.start()
    for c in g_rims:
        c.wait()
    for s in range(planes):
        for p in range(3):
            d = s - (p - 1)
            plane = grim[0] if d < 0 else grim[1] if d >= planes else g[d]
            g3[s, p * ch : (p + 1) * ch, :] = plane
    for c in x_copies:
        c.wait_recv()

    turn_and_shift(xg, xt)

    def weight_step(t, carry):
        total = None
        for s in range(planes):
            part = jnp.dot(
                g3[s],
                xt[lax.rem(t, 3), s, pl.ds(pl.multiple_of(lax.div(t, 3) * W, W), cells), :],
                preferred_element_type=F32,
            )
            total = part if total is None else total + part
        dwt[t] = total.T
        return carry

    lax.fori_loop(0, 9, weight_step, 0)
    d_copies = [
        to_slab(
            k,
            dwt.at[:, pl.ds(pl.multiple_of(lax.rem(me_s + k, S) * cs, cs), cs), :],
            dwr.at[k - 1], d_s, d_r, k - 1,
        )
        for k in range(1, S)
    ]
    for c in d_copies:
        c.start()
    conv(xt, wf, yx)
    x_rims = rims(yx.at[0, 2 * ch : 3 * ch, :], yx.at[planes - 1, 0:ch, :], xrim, xr_s, xr_r)
    for c in x_rims:
        c.start()

    for c in g_copies + w_copies:
        c.wait()
    turn_and_shift(gg, gt)
    conv(gt, wg, yg)
    i_rims = rims(yg.at[0, 2 * ch : 3 * ch, :], yg.at[planes - 1, 0:ch, :], irim, ir_s, ir_r)
    for c in i_rims:
        c.start()
    for c in x_rims:
        c.wait()
    finish(yx, xrim, feat)
    for c in d_copies:
        c.wait()
    total = dwt[:, pl.ds(pl.multiple_of(me_s * cs, cs), cs), :]
    for k in range(S - 1):
        total = total + dwr[k]
    dw[...] = total * factor
    for c in i_rims:
        c.wait()
    finish(yg, irim, igrad)


def local(inputs, filters, cotangent):
    S = lax.axis_size("slab")
    C = lax.axis_size("chan")
    ch, planes, cells = inputs.shape
    wide = C * ch
    cs = wide // S
    factor = 1.0 / math.sqrt(planes * S * cells)
    x = inputs.transpose(1, 0, 2)
    g = cotangent.transpose(1, 0, 2)
    taps = filters.reshape(3, 9, ch, wide)
    wf = taps.transpose(1, 3, 0, 2).reshape(9, wide, 3 * ch)
    back = filters[::-1].reshape(3, 9, ch, C, ch)
    wt = back.transpose(3, 1, 2, 0, 4).reshape(C, 9, ch, 3 * ch)
    dma = pltpu.SemaphoreType.DMA
    vmem = pl.BlockSpec(memory_space=pltpu.VMEM)
    feat, igrad, dw = pl.pallas_call(
        functools.partial(kernel, S, C, factor),
        out_shape=(
            jax.ShapeDtypeStruct((planes, ch, cells), BF16),
            jax.ShapeDtypeStruct((planes, ch, cells), BF16),
            jax.ShapeDtypeStruct((9, cs, 3 * ch), F32),
        ),
        in_specs=[vmem] * 4,
        out_specs=[vmem] * 3,
        scratch_shapes=[
            pltpu.VMEM((planes, wide, cells), BF16),
            pltpu.VMEM((planes, wide, cells), BF16),
            pltpu.VMEM((9, wide, 3 * ch), BF16),
            pltpu.VMEM((3, planes, cells + 2 * W, wide), BF16),
            pltpu.VMEM((3, planes, cells + 2 * W, wide), BF16),
            pltpu.VMEM((planes, 3 * ch, cells), F32),
            pltpu.VMEM((planes, 3 * ch, cells), F32),
            pltpu.VMEM((planes, 3 * ch, cells), BF16),
            pltpu.VMEM((2, ch, cells), BF16),
            pltpu.VMEM((2, ch, cells), F32),
            pltpu.VMEM((2, ch, cells), F32),
            pltpu.VMEM((9, wide, 3 * ch), F32),
            pltpu.VMEM((S - 1, 9, cs, 3 * ch), F32),
            dma((3,)),
            dma((C - 1,)), dma((C - 1,)),
            dma((C - 1,)), dma((C - 1,)),
            dma((C - 1,)), dma((C - 1,)),
            dma((2,)), dma((2,)),
            dma((2,)), dma((2,)),
            dma((2,)), dma((2,)),
            dma((S - 1,)), dma((S - 1,)),
        ],
        compiler_params=pltpu.CompilerParams(
            collective_id=0, has_side_effects=True, vmem_limit_bytes=48 * 1024 * 1024
        ),
    )(x, g, wf, wt)
    filter_grad = dw.reshape(3, 3, cs, 3, ch).transpose(3, 0, 1, 4, 2).reshape(27, ch, cs)
    return (feat.transpose(1, 0, 2), igrad.transpose(1, 0, 2), filter_grad)


def solution(mesh):
    placed = (P("chan", "slab", None), P(None, "chan", None), P("chan", "slab", None))
    return jax.shard_map(
        local,
        mesh=mesh,
        in_specs=placed,
        out_specs=(P("chan", "slab", None), P("chan", "slab", None), P(None, "chan", "slab")),
        check_vma=False,
    )
```

```python
import functools
import math

import jax
import jax.numpy as jnp
from jax import lax
from jax.experimental import pallas as pl
from jax.experimental.pallas import tpu as pltpu
from jax.sharding import PartitionSpec as P

W = 64
MESH = pl.DeviceIdType.MESH
F32 = jnp.float32
BF16 = jnp.bfloat16


def turn_and_shift(src, dst, s):
    cells = src.shape[2]

    def step(m, carry):
        turned = src[s, :, pl.ds(pl.multiple_of(m * 128, 128), 128)].astype(F32).T
        for h in range(128 // W):
            row = turned[h * W : (h + 1) * W]
            at = pl.ds(pl.multiple_of(m * 128 + (h + 1) * W, W), W)
            dst[0, s, at, :] = pltpu.roll(row, 1, 0).astype(BF16)
            dst[1, s, at, :] = row.astype(BF16)
            dst[2, s, at, :] = pltpu.roll(row, W - 1, 0).astype(BF16)
        return carry

    lax.fori_loop(0, cells // 128, step, 0)
    for r in range(3):
        dst[r, s, 0:W, :] = dst[r, s, cells : cells + W, :]
        dst[r, s, cells + W : cells + 2 * W, :] = dst[r, s, W : 2 * W, :]


def conv(src, weights, y, s):
    cells = y.shape[2]
    chunk = 512

    def step(n, carry):
        total = None
        for q in range(3):
            for r in range(3):
                part = jnp.dot(
                    src[r, s, pl.ds(pl.multiple_of(n * chunk + q * W, W), chunk), :],
                    weights[3 * q + r],
                    preferred_element_type=F32,
                )
                total = part if total is None else total + part
        y[s, :, pl.ds(pl.multiple_of(n * chunk, chunk), chunk)] = total.T
        return carry

    lax.fori_loop(0, cells // chunk, step, 0)


def finish(y, rim, out):
    planes = y.shape[0]
    ch = out.shape[1]
    for d in range(planes):
        total = y[d, ch : 2 * ch, :]
        total = total + (y[d - 1, 0:ch, :] if d > 0 else rim[0])
        total = total + (y[d + 1, 2 * ch : 3 * ch, :] if d < planes - 1 else rim[1])
        out[d] = total.astype(out.dtype)


def group_of(S):
    return next(n for n in (8, 4, 2, 1) if S % n == 0)


def kernel(
    S, C, factor,
    x, g, w,
    feat, igrad, dw,
    xg, gg, wf, wr, wg, xt, gt, yx, yg, g3, grim, xrim, irim, dwt, dwr,
    own_sem, xu_s, xu_r, xd_s, xd_r, gu_s, gu_r, gd_s, gd_r,
    w_s, w_r, v_s, v_r, a_s, a_r, gr_s, gr_r, xr_s, xr_r, ir_s, ir_r, d_s, d_r,
):
    planes, ch, cells = x.shape
    cs = dwt.shape[1] // S
    me_s = lax.axis_index("slab")
    me_c = lax.axis_index("chan")
    group = group_of(S)
    many = 8 // group
    base = lax.div(me_s, group) * group
    place = me_s - base

    barrier = pltpu.get_barrier_semaphore()
    for k in range(1, S):
        pl.semaphore_signal(barrier, inc=1, device_id={"slab": lax.rem(me_s + k, S)}, device_id_type=MESH)
    for k in range(1, C):
        pl.semaphore_signal(barrier, inc=1, device_id={"chan": lax.rem(me_c + k, C)}, device_id_type=MESH)
    pl.semaphore_wait(barrier, S - 1 + C - 1)

    def rows_of(j):
        return pl.ds(pl.multiple_of(j * ch, ch), ch)

    def to_chan(peer, src, dst, send, recv):
        return pltpu.make_async_remote_copy(
            src_ref=src, dst_ref=dst, send_sem=send, recv_sem=recv,
            device_id={"chan": peer}, device_id_type=MESH,
        )

    def to_slab(peer, src, dst, send, recv):
        return pltpu.make_async_remote_copy(
            src_ref=src, dst_ref=dst, send_sem=send, recv_sem=recv,
            device_id={"slab": peer}, device_id_type=MESH,
        )

    right, left = lax.rem(me_s + 1, S), lax.rem(me_s + S - 1, S)

    def low_rim(low, dst, send, recv):
        return to_slab(left, low, dst.at[1], send.at[1], recv.at[1])

    def high_rim(high, dst, send, recv):
        return to_slab(right, high, dst.at[0], send.at[0], recv.at[0])

    class Line:
        def __init__(self, src, dst, us, ur, ds, dr):
            self.src, self.dst, self.sems = src, dst, (us, ur, ds, dr)

        def up(self, s, h):
            rows = rows_of(lax.rem(me_c - (h - 1) + C, C))
            src = self.src.at[s] if h == 1 else self.dst.at[s, rows, :]
            us, ur, _, _ = self.sems
            return to_chan(
                lax.rem(me_c + 1, C), src, self.dst.at[s, rows, :], us.at[s, h - 1], ur.at[s, h - 1]
            )

        def down(self, s, h):
            rows = rows_of(lax.rem(me_c + h - 1, C))
            src = self.src.at[s] if h == 1 else self.dst.at[s, rows, :]
            _, _, ds, dr = self.sems
            return to_chan(
                lax.rem(me_c + C - 1, C), src, self.dst.at[s, rows, :], ds.at[s, h - 1], dr.at[s, h - 1]
            )

        def start(self, s):
            pl.when(me_c < C - 1)(lambda: self.up(s, 1).start())
            pl.when(me_c > 0)(lambda: self.down(s, 1).start())

        def hop(self, s, h):
            pl.when(me_c >= h)(lambda: self.up(s, h).wait_recv())
            if h < C - 1:
                pl.when((me_c >= h) & (me_c < C - 1))(lambda: self.up(s, h + 1).start())
            pl.when(me_c + h <= C - 1)(lambda: self.down(s, h).wait_recv())
            if h < C - 1:
                pl.when((me_c + h <= C - 1) & (me_c > 0))(lambda: self.down(s, h + 1).start())

        def drain(self, s):
            for h in range(1, C):
                pl.when((me_c >= h - 1) & (me_c < C - 1))(lambda h=h: self.up(s, h).wait_send())
                pl.when((me_c + h - 1 <= C - 1) & (me_c > 0))(lambda h=h: self.down(s, h).wait_send())

    xl = Line(x, xg, xu_s, xu_r, xd_s, xd_r)
    gl = Line(g, gg, gu_s, gu_r, gd_s, gd_r)
    mine = rows_of(me_c)
    hops = [(h, s) for h in range(1, C) for s in range(planes)]

    for s in range(planes):
        xl.start(s)
    g_rims = [
        low_rim(g.at[0], grim, gr_s, gr_r),
        high_rim(g.at[planes - 1], grim, gr_s, gr_r),
    ]
    for c in g_rims:
        c.start()
    own = [
        pltpu.make_async_copy(x, xg.at[:, mine, :], own_sem.at[0]),
        pltpu.make_async_copy(g, gg.at[:, mine, :], own_sem.at[1]),
    ]
    for c in own:
        c.start()

    def turn_weights(t, carry):
        both = jnp.concatenate([w[t], w[9 + t], w[18 + t]], axis=0)
        wf[t] = both.astype(F32).T.astype(BF16)
        return carry

    lax.fori_loop(0, 9, turn_weights, 0)
    block = pl.ds(place * many, many)
    w_copies = []
    for k in range(1, C):
        peer = lax.rem(me_c + k, C)
        w_copies += [
            to_chan(peer, wf.at[block, rows_of(peer), :], wr.at[me_c, block], w_s.at[k - 1], w_r.at[k - 1]),
            to_chan(peer, wf.at[8, rows_of(peer), :], wr.at[me_c, 8], v_s.at[k - 1], v_r.at[k - 1]),
        ]
    for c in w_copies:
        c.start()
    own_w = [
        pltpu.make_async_copy(wf.at[block, mine, :], wr.at[me_c, block], own_sem.at[2]),
        pltpu.make_async_copy(wf.at[8, mine, :], wr.at[me_c, 8], own_sem.at[3]),
    ]
    for c in own_w:
        c.start()
    for c in own + own_w:
        c.wait()
    waiting = list(hops)
    for _ in range(min(planes, len(waiting) - planes)):
        h, s = waiting.pop(0)
        xl.hop(s, h)
    for c in w_copies:
        c.wait()
    a_copies = [
        to_slab(
            base + lax.rem(place + k, group),
            wr.at[:, block], wr.at[:, block], a_s.at[k - 1], a_r.at[k - 1],
        )
        for k in range(1, group)
    ]
    for c in a_copies:
        c.start()
    for c in g_rims:
        c.wait()
    for s in range(planes):
        for p in range(3):
            d = s - (p - 1)
            plane = grim[0] if d < 0 else grim[1] if d >= planes else g[d]
            g3[s, p * ch : (p + 1) * ch, :] = plane
    while len(waiting) > planes:
        h, s = waiting.pop(0)
        xl.hop(s, h)
    for c in a_copies:
        c.wait()

    def place_weights(t, carry):
        for z in range(C):
            turned = wr[z, t].astype(F32).T
            parts = [turned[p * ch : (p + 1) * ch] for p in (2, 1, 0)]
            wg[8 - t, z * ch : (z + 1) * ch, :] = jnp.concatenate(parts, axis=1).astype(BF16)
        return carry

    lax.fori_loop(0, 9, place_weights, 0)

    for s in range(planes):
        h, _ = waiting.pop(0)
        xl.hop(s, h)
        if s == 0:
            for d in range(planes):
                gl.start(d)
        turn_and_shift(xg, xt, s)

    def weight_step(t, carry):
        total = None
        for s in range(planes):
            part = jnp.dot(
                g3[s],
                xt[lax.rem(t, 3), s, pl.ds(pl.multiple_of(lax.div(t, 3) * W, W), cells), :],
                preferred_element_type=F32,
            )
            total = part if total is None else total + part
        dwt[t] = total.T
        return carry

    waiting = list(hops)

    def next_hop():
        if len(waiting) > planes:
            h, s = waiting.pop(0)
            gl.hop(s, h)

    next_hop()
    for q in range(3):
        lax.fori_loop(3 * q, 3 * q + 3, weight_step, 0)
        next_hop()
    d_copies = []
    for k in range(1, S):
        peer = lax.rem(me_s + k, S)
        d_copies.append(
            to_slab(
                peer, dwt.at[:, pl.ds(pl.multiple_of(peer * cs, cs), cs), :],
                dwr.at[k - 1], d_s.at[k - 1], d_r.at[k - 1],
            )
        )
    for c in d_copies:
        c.start()
    x_rims = [
        low_rim(yx.at[0, 2 * ch : 3 * ch, :], xrim, xr_s, xr_r),
        high_rim(yx.at[planes - 1, 0:ch, :], xrim, xr_s, xr_r),
    ]
    for s in range(planes):
        conv(xt, wf, yx, s)
        if s == 0:
            x_rims[0].start()
        if s == planes - 1:
            x_rims[1].start()
        next_hop()
    while len(waiting) > planes:
        next_hop()
    i_rims = [
        low_rim(yg.at[0, 2 * ch : 3 * ch, :], irim, ir_s, ir_r),
        high_rim(yg.at[planes - 1, 0:ch, :], irim, ir_s, ir_r),
    ]
    for s in range(planes):
        h, _ = waiting.pop(0)
        gl.hop(s, h)
        turn_and_shift(gg, gt, s)
        conv(gt, wg, yg, s)
        if s == 0:
            i_rims[0].start()
        if s == planes - 1:
            i_rims[1].start()
    for c in x_rims:
        c.wait()
    finish(yx, xrim, feat)
    for c in d_copies:
        c.wait()
    total = dwt[:, pl.ds(pl.multiple_of(me_s * cs, cs), cs), :]
    for k in range(S - 1):
        total = total + dwr[k]
    total = total * factor
    for p in range(3):
        dw[9 * p : 9 * p + 9] = total[:, :, p * ch : (p + 1) * ch]
    for s in range(planes):
        xl.drain(s)
        gl.drain(s)
    for c in i_rims:
        c.wait()
    finish(yg, irim, igrad)


def local(inputs, filters, cotangent):
    S = lax.axis_size("slab")
    C = lax.axis_size("chan")
    ch, planes, cells = inputs.shape
    wide = C * ch
    cs = wide // S
    group = group_of(S)
    factor = 1.0 / math.sqrt(planes * S * cells)
    x = inputs.transpose(1, 0, 2)
    g = cotangent.transpose(1, 0, 2)
    dma = pltpu.SemaphoreType.DMA
    vmem = pl.BlockSpec(memory_space=pltpu.VMEM)
    feat, igrad, dw = pl.pallas_call(
        functools.partial(kernel, S, C, factor),
        out_shape=(
            jax.ShapeDtypeStruct((planes, ch, cells), BF16),
            jax.ShapeDtypeStruct((planes, ch, cells), BF16),
            jax.ShapeDtypeStruct((27, cs, ch), F32),
        ),
        in_specs=[vmem] * 3,
        out_specs=[vmem] * 3,
        scratch_shapes=[
            pltpu.VMEM((planes, wide, cells), BF16),
            pltpu.VMEM((planes, wide, cells), BF16),
            pltpu.VMEM((9, wide, 3 * ch), BF16),
            pltpu.VMEM((C, 9, ch, 3 * ch), BF16),
            pltpu.VMEM((9, wide, 3 * ch), BF16),
            pltpu.VMEM((3, planes, cells + 2 * W, wide), BF16),
            pltpu.VMEM((3, planes, cells + 2 * W, wide), BF16),
            pltpu.VMEM((planes, 3 * ch, cells), F32),
            pltpu.VMEM((planes, 3 * ch, cells), F32),
            pltpu.VMEM((planes, 3 * ch, cells), BF16),
            pltpu.VMEM((2, ch, cells), BF16),
            pltpu.VMEM((2, ch, cells), F32),
            pltpu.VMEM((2, ch, cells), F32),
            pltpu.VMEM((9, wide, 3 * ch), F32),
            pltpu.VMEM((S - 1, 9, cs, 3 * ch), F32),
            dma((4,)),
        ]
        + [dma((planes, C - 1))] * 8
        + [dma((C - 1,))] * 4
        + [dma((max(group - 1, 1),))] * 2
        + [dma((2,))] * 6
        + [dma((S - 1,))] * 2,
        compiler_params=pltpu.CompilerParams(
            collective_id=0, has_side_effects=True, vmem_limit_bytes=48 * 1024 * 1024
        ),
    )(x, g, filters)
    return (feat.transpose(1, 0, 2), igrad.transpose(1, 0, 2), dw.transpose(0, 2, 1))


def solution(mesh):
    placed = (P("chan", "slab", None), P(None, "chan", None), P("chan", "slab", None))
    return jax.shard_map(
        local,
        mesh=mesh,
        in_specs=placed,
        out_specs=(P("chan", "slab", None), P("chan", "slab", None), P(None, "chan", "slab")),
        check_vma=False,
    )
```

```python
import functools
import math

import jax
import jax.numpy as jnp
from jax import lax
from jax.experimental import pallas as pl
from jax.experimental.pallas import tpu as pltpu
from jax.sharding import PartitionSpec as P

W = 64
CHUNK = 512
MESH = pl.DeviceIdType.MESH
F32 = jnp.float32
BF16 = jnp.bfloat16


def turn_and_shift(src, dst, s):
    cells = src.shape[2]

    def step(m, carry):
        turned = src[s, :, pl.ds(pl.multiple_of(m * 128, 128), 128)].astype(F32).T
        for h in range(128 // W):
            row = turned[h * W : (h + 1) * W]
            at = pl.ds(pl.multiple_of(m * 128 + (h + 1) * W, W), W)
            dst[0, s, at, :] = pltpu.roll(row, 1, 0).astype(BF16)
            dst[1, s, at, :] = row.astype(BF16)
            dst[2, s, at, :] = pltpu.roll(row, W - 1, 0).astype(BF16)
        return carry

    lax.fori_loop(0, cells // 128, step, 0)
    for r in range(3):
        dst[r, s, 0:W, :] = dst[r, s, cells : cells + W, :]
        dst[r, s, cells + W : cells + 2 * W, :] = dst[r, s, W : 2 * W, :]


def conv(src, weights, partial, y, s, after):
    planes = weights.shape[0]
    cells = partial.shape[0]
    chunk = CHUNK

    def step(n, carry):
        here = pl.ds(pl.multiple_of(n * chunk, chunk), chunk)
        total = None if s == 0 else partial[here, :]
        for q in range(3):
            for r in range(3):
                part = jnp.dot(
                    src[r, s, pl.ds(pl.multiple_of(n * chunk + q * W, W), chunk), :],
                    weights[s, 3 * q + r],
                    preferred_element_type=F32,
                )
                total = part if total is None else total + part
        if s < planes - 1:
            partial[here, :] = total
        else:
            y[:, here] = total.T
            after(n)
        return carry

    lax.fori_loop(0, cells // chunk, step, 0)


def finish(y, rim, out, n):
    planes, ch, _ = out.shape
    here = slice(n * CHUNK, (n + 1) * CHUNK)
    for d in range(planes):
        total = y[(d + 1) * ch : (d + 2) * ch, here]
        if d == 0:
            total = total + rim[0, :, here]
        if d == planes - 1:
            total = total + rim[1, :, here]
        out[d, :, here] = total.astype(out.dtype)


def set_apart(blocks, s, planes, axis):
    ch = blocks[0].shape[axis]
    shape = list(blocks[0].shape)
    parts = list(blocks)
    if s > 0:
        shape[axis] = s * ch
        parts = [jnp.zeros(shape, F32)] + parts
    if s < planes - 1:
        shape[axis] = (planes - 1 - s) * ch
        parts = parts + [jnp.zeros(shape, F32)]
    return jnp.concatenate(parts, axis=axis)


def group_of(S):
    return next(n for n in (8, 4, 2, 1) if S % n == 0)


def kernel(
    S, C, factor,
    x, g, w,
    feat, igrad, dw,
    xg, gg, wf, ws, wr, wg, xt, gt, px, pg, yx, yg, g3, grim, xrim, irim, dwa, dwt, dwr,
    own_sem, xu_s, xu_r, xd_s, xd_r, gu_s, gu_r, gd_s, gd_r,
    w_s, w_r, v_s, v_r, a_s, a_r, gr_s, gr_r, xr_s, xr_r, ir_s, ir_r, d_s, d_r,
):
    planes, ch, cells = x.shape
    cs = dwt.shape[1] // S
    me_s = lax.axis_index("slab")
    me_c = lax.axis_index("chan")
    group = group_of(S)
    many = 8 // group
    base = lax.div(me_s, group) * group
    place = me_s - base

    barrier = pltpu.get_barrier_semaphore()
    for k in range(1, S):
        pl.semaphore_signal(barrier, inc=1, device_id={"slab": lax.rem(me_s + k, S)}, device_id_type=MESH)
    for k in range(1, C):
        pl.semaphore_signal(barrier, inc=1, device_id={"chan": lax.rem(me_c + k, C)}, device_id_type=MESH)
    pl.semaphore_wait(barrier, S - 1 + C - 1)

    def rows_of(j):
        return pl.ds(pl.multiple_of(j * ch, ch), ch)

    def to_chan(peer, src, dst, send, recv):
        return pltpu.make_async_remote_copy(
            src_ref=src, dst_ref=dst, send_sem=send, recv_sem=recv,
            device_id={"chan": peer}, device_id_type=MESH,
        )

    def to_slab(peer, src, dst, send, recv):
        return pltpu.make_async_remote_copy(
            src_ref=src, dst_ref=dst, send_sem=send, recv_sem=recv,
            device_id={"slab": peer}, device_id_type=MESH,
        )

    right, left = lax.rem(me_s + 1, S), lax.rem(me_s + S - 1, S)

    class Unit:
        def __init__(self, src, dst, s, us, ur, ds, dr):
            self.src, self.dst, self.s = src, dst, s
            self.sems = ((1, us, ur), (-1, ds, dr))

        def copy(self, way, send, recv, h, origin):
            rows = rows_of(lax.rem(me_c - way * origin + C, C))
            dst = self.dst.at[self.s, rows, :]
            src = self.src.at[self.s] if origin == 0 else dst
            peer = lax.rem(me_c + way * (h - origin) + C, C)
            return to_chan(peer, src, dst, send.at[self.s, h - 1], recv.at[self.s, h - 1])

        def sends(self, act, origin):
            for h in (origin + 2, origin + 1):
                if h > C - 1:
                    continue
                for way, send, recv in self.sems:
                    first, last = me_c - way * origin, me_c + way * (h - origin)
                    ok = (first >= 0) & (first <= C - 1) & (last >= 0) & (last <= C - 1)
                    pl.when(ok)(lambda c=self.copy(way, send, recv, h, origin): act(c))

        def take(self, h):
            for way, send, recv in self.sems:
                first = me_c - way * h
                pl.when((first >= 0) & (first <= C - 1))(
                    lambda c=self.copy(way, send, recv, h, h): c.wait_recv()
                )

        def start(self):
            self.sends(lambda c: c.start(), 0)

        def relay(self):
            for h in range(2, C - 1, 2):
                self.take(h)
                self.sends(lambda c: c.start(), h)

        def rest(self):
            for h in range(1, C):
                if h % 2 == 1 or h >= C - 1:
                    self.take(h)

        def drain(self):
            for origin in range(0, C - 1, 2):
                self.sends(lambda c: c.wait_send(), origin)

    xu = [Unit(x, xg, s, xu_s, xu_r, xd_s, xd_r) for s in range(planes)]
    gu = [Unit(g, gg, s, gu_s, gu_r, gd_s, gd_r) for s in range(planes)]
    units = xu + gu
    mine = rows_of(me_c)

    units[0].start()
    g_rims = [
        to_slab(left, g.at[0], grim.at[1], gr_s.at[1], gr_r.at[1]),
        to_slab(right, g.at[planes - 1], grim.at[0], gr_s.at[0], gr_r.at[0]),
    ]
    for c in g_rims:
        c.start()
    own = [
        pltpu.make_async_copy(x, xg.at[:, mine, :], own_sem.at[0]),
        pltpu.make_async_copy(g, gg.at[:, mine, :], own_sem.at[1]),
    ]
    for c in own:
        c.start()

    def turn_weights(t, carry):
        blocks = [w[18 + t].astype(F32), w[9 + t].astype(F32), w[t].astype(F32)]
        for s in range(planes):
            turned = set_apart(blocks, s, planes, 0).T.astype(BF16)
            wf[s, t] = turned
            if s == 0:
                ws[t] = turned[:, : 3 * ch]
        return carry

    lax.fori_loop(0, 9, turn_weights, 0)
    units[0].relay()
    units[1].start()
    block = pl.ds(place * many, many)
    w_copies = []
    for k in range(1, C):
        peer = lax.rem(me_c + k, C)
        w_copies += [
            to_chan(peer, ws.at[block, rows_of(peer), :], wr.at[me_c, block], w_s.at[k - 1], w_r.at[k - 1]),
            to_chan(peer, ws.at[8, rows_of(peer), :], wr.at[me_c, 8], v_s.at[k - 1], v_r.at[k - 1]),
        ]
    for c in w_copies:
        c.start()
    own += [
        pltpu.make_async_copy(ws.at[block, mine, :], wr.at[me_c, block], own_sem.at[2]),
        pltpu.make_async_copy(ws.at[8, mine, :], wr.at[me_c, 8], own_sem.at[3]),
    ]
    for c in own[2:]:
        c.start()
    for c in own:
        c.wait()
    for c in g_rims:
        c.wait()
    for s in range(planes):
        for p in range(3):
            d = s - (p - 1)
            plane = grim[0] if d < 0 else grim[1] if d >= planes else g[d]
            g3[s, p * ch : (p + 1) * ch, :] = plane

    def weight_step(s, t, carry):
        total = jnp.dot(
            g3[s],
            xt[lax.rem(t, 3), s, pl.ds(pl.multiple_of(lax.div(t, 3) * W, W), cells), :],
            preferred_element_type=F32,
        )
        if s > 0:
            total = total + dwa[t]
        if s < planes - 1:
            dwa[t] = total
        else:
            dwt[t] = total.T
        return carry

    def x_rim(n):
        return rim_copies(yx, xrim, xr_s, xr_r, n)

    def i_rim(n):
        return rim_copies(yg, irim, ir_s, ir_r, n)

    def rim_copies(y, rim, send, recv, n):
        here = pl.ds(n * CHUNK if isinstance(n, int) else pl.multiple_of(n * CHUNK, CHUNK), CHUNK)
        return [
            to_slab(left, y.at[0:ch, here], rim.at[1, :, here], send.at[1, n], recv.at[1, n]),
            to_slab(
                right, y.at[(planes + 1) * ch : (planes + 2) * ch, here], rim.at[0, :, here],
                send.at[0, n], recv.at[0, n],
            ),
        ]

    def start_all(copies):
        for c in copies:
            c.start()

    a_copies = [
        to_slab(
            base + lax.rem(place + k, group),
            wr.at[:, block], wr.at[:, block], a_s.at[k - 1], a_r.at[k - 1],
        )
        for k in range(1, group)
    ]
    d_copies = []
    for k in range(1, S):
        peer = lax.rem(me_s + k, S)
        d_copies.append(
            to_slab(
                peer, dwt.at[:, pl.ds(pl.multiple_of(peer * cs, cs), cs), :],
                dwr.at[k - 1], d_s.at[k - 1], d_r.at[k - 1],
            )
        )

    def place_weights(t, carry):
        for z in range(C):
            turned = wr[z, t].astype(F32).T
            parts = [turned[p * ch : (p + 1) * ch] for p in (2, 1, 0)]
            for s in range(planes):
                wg[s, 8 - t, z * ch : (z + 1) * ch, :] = set_apart(parts, s, planes, 1).astype(BF16)
        return carry

    def go_on(i):
        if i < len(units):
            units[i].relay()
        if i + 1 < len(units):
            units[i + 1].start()

    for s in range(planes):
        units[s].rest()
        turn_and_shift(xg, xt, s)
        lax.fori_loop(0, 9, functools.partial(weight_step, s), 0)
        if s == planes - 1:
            start_all(d_copies)
        go_on(s + 1)
        conv(xt, wf, px, yx, s, lambda n: start_all(x_rim(n)))
        if s == 0:
            for c in w_copies:
                c.wait()
            start_all(a_copies)
    for c in a_copies:
        c.wait()
    lax.fori_loop(0, 9, place_weights, 0)
    chunks = cells // CHUNK
    for s in range(planes):
        units[planes + s].rest()
        turn_and_shift(gg, gt, s)
        go_on(planes + s + 1)
        conv(gt, wg, pg, yg, s, lambda n: start_all(i_rim(n)))
        if s == 0:
            for n in range(chunks):
                for c in x_rim(n):
                    c.wait()
                finish(yx, xrim, feat, n)
            for c in d_copies:
                c.wait()
            total = dwt[:, pl.ds(pl.multiple_of(me_s * cs, cs), cs), :]
            for k in range(S - 1):
                total = total + dwr[k]
            total = total * factor
            for p in range(3):
                dw[9 * p : 9 * p + 9] = total[:, :, p * ch : (p + 1) * ch]
    for u in units:
        u.drain()
    for n in range(chunks):
        for c in i_rim(n):
            c.wait()
        finish(yg, irim, igrad, n)


def local(inputs, filters, cotangent):
    S = lax.axis_size("slab")
    C = lax.axis_size("chan")
    ch, planes, cells = inputs.shape
    wide = C * ch
    cs = wide // S
    group = group_of(S)
    spread = (planes + 2) * ch
    factor = 1.0 / math.sqrt(planes * S * cells)
    x = inputs.transpose(1, 0, 2)
    g = cotangent.transpose(1, 0, 2)
    dma = pltpu.SemaphoreType.DMA
    vmem = pl.BlockSpec(memory_space=pltpu.VMEM)
    feat, igrad, dw = pl.pallas_call(
        functools.partial(kernel, S, C, factor),
        out_shape=(
            jax.ShapeDtypeStruct((planes, ch, cells), BF16),
            jax.ShapeDtypeStruct((planes, ch, cells), BF16),
            jax.ShapeDtypeStruct((27, cs, ch), F32),
        ),
        in_specs=[vmem] * 3,
        out_specs=[vmem] * 3,
        scratch_shapes=[
            pltpu.VMEM((planes, wide, cells), BF16),
            pltpu.VMEM((planes, wide, cells), BF16),
            pltpu.VMEM((planes, 9, wide, spread), BF16),
            pltpu.VMEM((9, wide, 3 * ch), BF16),
            pltpu.VMEM((C, 9, ch, 3 * ch), BF16),
            pltpu.VMEM((planes, 9, wide, spread), BF16),
            pltpu.VMEM((3, planes, cells + 2 * W, wide), BF16),
            pltpu.VMEM((3, planes, cells + 2 * W, wide), BF16),
            pltpu.VMEM((cells, spread), F32),
            pltpu.VMEM((cells, spread), F32),
            pltpu.VMEM((spread, cells), F32),
            pltpu.VMEM((spread, cells), F32),
            pltpu.VMEM((planes, 3 * ch, cells), BF16),
            pltpu.VMEM((2, ch, cells), BF16),
            pltpu.VMEM((2, ch, cells), F32),
            pltpu.VMEM((2, ch, cells), F32),
            pltpu.VMEM((9, 3 * ch, wide), F32),
            pltpu.VMEM((9, wide, 3 * ch), F32),
            pltpu.VMEM((S - 1, 9, cs, 3 * ch), F32),
            dma((4,)),
        ]
        + [dma((planes, C - 1))] * 8
        + [dma((C - 1,))] * 4
        + [dma((max(group - 1, 1),))] * 2
        + [dma((2,))] * 2
        + [dma((2, cells // CHUNK))] * 4
        + [dma((S - 1,))] * 2,
        compiler_params=pltpu.CompilerParams(
            collective_id=0, has_side_effects=True, vmem_limit_bytes=48 * 1024 * 1024
        ),
    )(x, g, filters)
    return (feat.transpose(1, 0, 2), igrad.transpose(1, 0, 2), dw.transpose(0, 2, 1))


def solution(mesh):
    placed = (P("chan", "slab", None), P(None, "chan", None), P("chan", "slab", None))
    return jax.shard_map(
        local,
        mesh=mesh,
        in_specs=placed,
        out_specs=(P("chan", "slab", None), P("chan", "slab", None), P(None, "chan", "slab")),
        check_vma=False,
    )
```

```python
import functools
import math

import jax
import jax.numpy as jnp
from jax import lax
from jax.experimental import pallas as pl
from jax.experimental.pallas import tpu as pltpu
from jax.sharding import PartitionSpec as P

W = 64
CHUNK = 512
MESH = pl.DeviceIdType.MESH
F32 = jnp.float32
BF16 = jnp.bfloat16


def turn_and_shift(src, dst, s):
    cells = src.shape[2]

    def step(m, carry):
        turned = src[s, :, pl.ds(pl.multiple_of(m * 128, 128), 128)].T.astype(F32)
        for h in range(128 // W):
            row = turned[h * W : (h + 1) * W]
            at = pl.ds(pl.multiple_of(m * 128 + (h + 1) * W, W), W)
            dst[0, s, at, :] = pltpu.roll(row, 1, 0).astype(BF16)
            dst[1, s, at, :] = row.astype(BF16)
            dst[2, s, at, :] = pltpu.roll(row, W - 1, 0).astype(BF16)
        return carry

    lax.fori_loop(0, cells // 128, step, 0, unroll=4)
    for r in range(3):
        dst[r, s, 0:W, :] = dst[r, s, cells : cells + W, :]
        dst[r, s, cells + W : cells + 2 * W, :] = dst[r, s, W : 2 * W, :]


def conv(src, weights, partial, y, s, after):
    planes = weights.shape[0]
    cells = partial.shape[0]
    chunk = CHUNK

    def step(n, carry):
        here = pl.ds(pl.multiple_of(n * chunk, chunk), chunk)
        total = None if s == 0 else partial[here, :]
        for q in range(3):
            for r in range(3):
                part = jnp.dot(
                    src[r, s, pl.ds(pl.multiple_of(n * chunk + q * W, W), chunk), :],
                    weights[s, 3 * q + r],
                    preferred_element_type=F32,
                )
                total = part if total is None else total + part
        if s < planes - 1:
            partial[here, :] = total
        else:
            y[:, here] = total.T
            after(n)
        return carry

    lax.fori_loop(0, cells // chunk, step, 0)


def finish(y, rim, out, n):
    planes, ch, _ = out.shape
    here = slice(n * CHUNK, (n + 1) * CHUNK)
    for d in range(planes):
        total = y[(d + 1) * ch : (d + 2) * ch, here]
        if d == 0:
            total = total + rim[0, :, here]
        if d == planes - 1:
            total = total + rim[1, :, here]
        out[d, :, here] = total.astype(out.dtype)


def moved(v, by):
    if by == 0:
        return v
    return jnp.concatenate([v[:, v.shape[1] - by :], v[:, : v.shape[1] - by]], axis=1)


def group_of(S):
    return next(n for n in (8, 4, 2, 1) if S % n == 0)


def kernel(
    S, C, factor,
    x, g, w,
    feat, igrad, dw,
    xg, gg, wf, we, wg, xt, gt, px, pg, yx, yg, g3, grim, xrim, irim, dwa, dwt, dwr,
    own_sem, xu_s, xu_r, xd_s, xd_r, gu_s, gu_r, gd_s, gd_r,
    w_s, w_r, v_s, v_r, a_s, a_r, gr_s, gr_r, xr_s, xr_r, ir_s, ir_r, d_s, d_r,
):
    planes, ch, cells = x.shape
    cs = dwt.shape[1] // S
    me_s = lax.axis_index("slab")
    me_c = lax.axis_index("chan")
    group = group_of(S)
    many = 8 // group
    base = lax.div(me_s, group) * group
    place = me_s - base

    barrier = pltpu.get_barrier_semaphore()
    for k in range(1, S):
        pl.semaphore_signal(barrier, inc=1, device_id={"slab": lax.rem(me_s + k, S)}, device_id_type=MESH)
    for k in range(1, C):
        pl.semaphore_signal(barrier, inc=1, device_id={"chan": lax.rem(me_c + k, C)}, device_id_type=MESH)
    pl.semaphore_wait(barrier, S - 1 + C - 1)

    def rows_of(j):
        return pl.ds(pl.multiple_of(j * ch, ch), ch)

    def to_chan(peer, src, dst, send, recv):
        return pltpu.make_async_remote_copy(
            src_ref=src, dst_ref=dst, send_sem=send, recv_sem=recv,
            device_id={"chan": peer}, device_id_type=MESH,
        )

    def to_slab(peer, src, dst, send, recv):
        return pltpu.make_async_remote_copy(
            src_ref=src, dst_ref=dst, send_sem=send, recv_sem=recv,
            device_id={"slab": peer}, device_id_type=MESH,
        )

    right, left = lax.rem(me_s + 1, S), lax.rem(me_s + S - 1, S)

    class Unit:
        def __init__(self, src, dst, s, us, ur, ds, dr):
            self.src, self.dst, self.s = src, dst, s
            self.sems = ((1, us, ur), (-1, ds, dr))

        def copy(self, way, send, recv, h, origin):
            rows = rows_of(lax.rem(me_c - way * origin + C, C))
            dst = self.dst.at[self.s, rows, :]
            src = self.src.at[self.s] if origin == 0 else dst
            peer = lax.rem(me_c + way * (h - origin) + C, C)
            return to_chan(peer, src, dst, send.at[self.s, h - 1], recv.at[self.s, h - 1])

        def sends(self, act, origin):
            for h in (origin + 2, origin + 1):
                if h > C - 1:
                    continue
                for way, send, recv in self.sems:
                    first, last = me_c - way * origin, me_c + way * (h - origin)
                    ok = (first >= 0) & (first <= C - 1) & (last >= 0) & (last <= C - 1)
                    pl.when(ok)(lambda c=self.copy(way, send, recv, h, origin): act(c))

        def take(self, h):
            for way, send, recv in self.sems:
                first = me_c - way * h
                pl.when((first >= 0) & (first <= C - 1))(
                    lambda c=self.copy(way, send, recv, h, h): c.wait_recv()
                )

        def start(self):
            self.sends(lambda c: c.start(), 0)

        def relay(self):
            for h in range(2, C - 1, 2):
                self.take(h)
                self.sends(lambda c: c.start(), h)

        def rest(self):
            for h in range(1, C):
                if h % 2 == 1 or h >= C - 1:
                    self.take(h)

        def drain(self):
            for origin in range(0, C - 1, 2):
                self.sends(lambda c: c.wait_send(), origin)

    xu = [Unit(x, xg, s, xu_s, xu_r, xd_s, xd_r) for s in range(planes)]
    gu = [Unit(g, gg, s, gu_s, gu_r, gd_s, gd_r) for s in range(planes)]
    units = xu + gu
    mine = rows_of(me_c)

    units[0].start()
    g_rims = [
        to_slab(left, g.at[0], grim.at[1], gr_s.at[1], gr_r.at[1]),
        to_slab(right, g.at[planes - 1], grim.at[0], gr_s.at[0], gr_r.at[0]),
    ]
    for c in g_rims:
        c.start()
    own = [
        pltpu.make_async_copy(x, xg.at[:, mine, :], own_sem.at[0]),
        pltpu.make_async_copy(g, gg.at[:, mine, :], own_sem.at[1]),
    ]
    for c in own:
        c.start()

    blank = [jnp.zeros((ch, (planes - 1) * ch), F32)] if planes > 1 else []

    def split_weights(t, carry):
        taps = [w[9 * p + t].astype(F32) for p in range(3)]
        for z in range(C):
            parts = [tap[:, z * ch : (z + 1) * ch] for tap in taps] + blank
            we[z, 8 - t] = jnp.concatenate(parts, axis=1).astype(BF16)
        return carry

    lax.fori_loop(0, 9, split_weights, 0)
    block = pl.ds(place * many, many)
    w_copies = []
    for k in range(1, C):
        peer = lax.rem(me_c + k, C)
        w_copies += [
            to_chan(peer, we.at[peer, block], wg.at[0, block, mine, :], w_s.at[k - 1], w_r.at[k - 1]),
            to_chan(peer, we.at[peer, 8], wg.at[0, 8, mine, :], v_s.at[k - 1], v_r.at[k - 1]),
        ]
    for c in w_copies:
        c.start()
    own += [
        pltpu.make_async_copy(we.at[me_c, block], wg.at[0, block, mine, :], own_sem.at[2]),
        pltpu.make_async_copy(we.at[me_c, 8], wg.at[0, 8, mine, :], own_sem.at[3]),
    ]
    for c in own[2:]:
        c.start()

    def turn_weights(t, carry):
        blocks = [w[9 * p + t].astype(F32) for p in (2, 1, 0)]
        if planes > 1:
            blocks.append(jnp.zeros(((planes - 1) * ch, C * ch), F32))
        turned = jnp.concatenate(blocks, axis=0).T
        for s in range(planes):
            wf[s, t] = moved(turned, s * ch).astype(BF16)
        return carry

    lax.fori_loop(0, 9, turn_weights, 0)
    units[0].relay()
    units[1].start()
    for c in own:
        c.wait()
    for c in g_rims:
        c.wait()
    for s in range(planes):
        for p in range(3):
            d = s - (p - 1)
            plane = grim[0] if d < 0 else grim[1] if d >= planes else g[d]
            g3[s, p * ch : (p + 1) * ch, :] = plane
    a_copies = [
        to_slab(
            base + lax.rem(place + k, group),
            wg.at[0, block], wg.at[0, block], a_s.at[k - 1], a_r.at[k - 1],
        )
        for k in range(1, group)
    ]
    for c in w_copies:
        c.wait()
    for c in a_copies:
        c.start()

    def weight_step(s, t, carry):
        total = jnp.dot(
            g3[s],
            xt[lax.rem(t, 3), s, pl.ds(pl.multiple_of(lax.div(t, 3) * W, W), cells), :],
            preferred_element_type=F32,
        )
        if s > 0:
            total = total + dwa[t]
        if s < planes - 1:
            dwa[t] = total
        else:
            dwt[t] = total.T
        return carry

    def x_rim(n):
        return rim_copies(yx, xrim, xr_s, xr_r, n)

    def i_rim(n):
        return rim_copies(yg, irim, ir_s, ir_r, n)

    def rim_copies(y, rim, send, recv, n):
        here = pl.ds(n * CHUNK if isinstance(n, int) else pl.multiple_of(n * CHUNK, CHUNK), CHUNK)
        return [
            to_slab(left, y.at[0:ch, here], rim.at[1, :, here], send.at[1, n], recv.at[1, n]),
            to_slab(
                right, y.at[(planes + 1) * ch : (planes + 2) * ch, here], rim.at[0, :, here],
                send.at[0, n], recv.at[0, n],
            ),
        ]

    def start_all(copies):
        for c in copies:
            c.start()

    d_copies = []
    for k in range(1, S):
        peer = lax.rem(me_s + k, S)
        d_copies.append(
            to_slab(
                peer, dwt.at[:, pl.ds(pl.multiple_of(peer * cs, cs), cs), :],
                dwr.at[k - 1], d_s.at[k - 1], d_r.at[k - 1],
            )
        )

    def place_weights(t, carry):
        v = wg[0, t].astype(F32)
        for s in range(1, planes):
            wg[s, t] = moved(v, s * ch).astype(BF16)
        return carry

    def relay(i):
        if i < len(units):
            units[i].relay()

    def rest(i):
        units[i].rest()
        if i + 2 < len(units):
            units[i + 2].start()

    for s in range(planes):
        rest(s)
        turn_and_shift(xg, xt, s)
        lax.fori_loop(0, 9, functools.partial(weight_step, s), 0)
        if s == planes - 1:
            start_all(d_copies)
        relay(s + 1)
        conv(xt, wf, px, yx, s, lambda n: start_all(x_rim(n)))
        if s == 0:
            for c in a_copies:
                c.wait()
            lax.fori_loop(0, 9, place_weights, 0)
    chunks = cells // CHUNK
    for s in range(planes):
        rest(planes + s)
        turn_and_shift(gg, gt, s)
        relay(planes + s + 1)
        conv(gt, wg, pg, yg, s, lambda n: start_all(i_rim(n)))
        if s == 0:
            for n in range(chunks):
                for c in x_rim(n):
                    c.wait()
                finish(yx, xrim, feat, n)
            for c in d_copies:
                c.wait()
            total = dwt[:, pl.ds(pl.multiple_of(me_s * cs, cs), cs), :]
            for k in range(S - 1):
                total = total + dwr[k]
            total = total * factor
            for p in range(3):
                dw[9 * p : 9 * p + 9] = total[:, :, p * ch : (p + 1) * ch]
    for u in units:
        u.drain()
    for n in range(chunks):
        for c in i_rim(n):
            c.wait()
        finish(yg, irim, igrad, n)


def local(inputs, filters, cotangent):
    S = lax.axis_size("slab")
    C = lax.axis_size("chan")
    ch, planes, cells = inputs.shape
    wide = C * ch
    cs = wide // S
    group = group_of(S)
    spread = (planes + 2) * ch
    factor = 1.0 / math.sqrt(planes * S * cells)
    x = inputs.transpose(1, 0, 2)
    g = cotangent.transpose(1, 0, 2)
    dma = pltpu.SemaphoreType.DMA
    vmem = pl.BlockSpec(memory_space=pltpu.VMEM)
    feat, igrad, dw = pl.pallas_call(
        functools.partial(kernel, S, C, factor),
        out_shape=(
            jax.ShapeDtypeStruct((planes, ch, cells), BF16),
            jax.ShapeDtypeStruct((planes, ch, cells), BF16),
            jax.ShapeDtypeStruct((27, cs, ch), F32),
        ),
        in_specs=[vmem] * 3,
        out_specs=[vmem] * 3,
        scratch_shapes=[
            pltpu.VMEM((planes, wide, cells), BF16),
            pltpu.VMEM((planes, wide, cells), BF16),
            pltpu.VMEM((planes, 9, wide, spread), BF16),
            pltpu.VMEM((C, 9, ch, spread), BF16),
            pltpu.VMEM((planes, 9, wide, spread), BF16),
            pltpu.VMEM((3, planes, cells + 2 * W, wide), BF16),
            pltpu.VMEM((3, planes, cells + 2 * W, wide), BF16),
            pltpu.VMEM((cells, spread), F32),
            pltpu.VMEM((cells, spread), F32),
            pltpu.VMEM((spread, cells), F32),
            pltpu.VMEM((spread, cells), F32),
            pltpu.VMEM((planes, 3 * ch, cells), BF16),
            pltpu.VMEM((2, ch, cells), BF16),
            pltpu.VMEM((2, ch, cells), F32),
            pltpu.VMEM((2, ch, cells), F32),
            pltpu.VMEM((9, 3 * ch, wide), F32),
            pltpu.VMEM((9, wide, 3 * ch), F32),
            pltpu.VMEM((S - 1, 9, cs, 3 * ch), F32),
            dma((4,)),
        ]
        + [dma((planes, C - 1))] * 8
        + [dma((C - 1,))] * 4
        + [dma((max(group - 1, 1),))] * 2
        + [dma((2,))] * 2
        + [dma((2, cells // CHUNK))] * 4
        + [dma((S - 1,))] * 2,
        compiler_params=pltpu.CompilerParams(
            collective_id=0, has_side_effects=True, vmem_limit_bytes=48 * 1024 * 1024
        ),
    )(x, g, filters)
    return (feat.transpose(1, 0, 2), igrad.transpose(1, 0, 2), dw.transpose(0, 2, 1))


def solution(mesh):
    placed = (P("chan", "slab", None), P(None, "chan", None), P("chan", "slab", None))
    return jax.shard_map(
        local,
        mesh=mesh,
        in_specs=placed,
        out_specs=(P("chan", "slab", None), P("chan", "slab", None), P(None, "chan", "slab")),
        check_vma=False,
    )
```

```python
import functools
import math

import jax
import jax.numpy as jnp
from jax import lax
from jax.experimental import pallas as pl
from jax.experimental.pallas import tpu as pltpu
from jax.sharding import PartitionSpec as P

W = 64
CHUNK = 512
MESH = pl.DeviceIdType.MESH
F32 = jnp.float32
BF16 = jnp.bfloat16


def turn_and_shift(src, dst, s):
    cells = src.shape[2]

    def step(m, carry):
        turned = src[s, :, pl.ds(pl.multiple_of(m * 128, 128), 128)].T.astype(F32)
        for h in range(128 // W):
            row = turned[h * W : (h + 1) * W]
            at = pl.ds(pl.multiple_of(m * 128 + (h + 1) * W, W), W)
            dst[0, s, at, :] = pltpu.roll(row, 1, 0).astype(BF16)
            dst[1, s, at, :] = row.astype(BF16)
            dst[2, s, at, :] = pltpu.roll(row, W - 1, 0).astype(BF16)
        return carry

    lax.fori_loop(0, cells // 128, step, 0, unroll=4)
    for r in range(3):
        dst[r, s, 0:W, :] = dst[r, s, cells : cells + W, :]
        dst[r, s, cells + W : cells + 2 * W, :] = dst[r, s, W : 2 * W, :]


def conv(src, weights, partial, y, s, after):
    planes = weights.shape[0]
    cells, spread = partial.shape
    ch = spread // (planes + 2)
    chunk = CHUNK

    def step(n, carry):
        here = pl.ds(pl.multiple_of(n * chunk, chunk), chunk)
        total = None if s == 0 else partial[here, :]
        for q in range(3):
            for r in range(3):
                part = jnp.dot(
                    src[r, s, pl.ds(pl.multiple_of(n * chunk + q * W, W), chunk), :],
                    weights[s, 3 * q + r],
                    preferred_element_type=F32,
                )
                total = part if total is None else total + part
        if s < planes - 1:
            partial[here, :] = total
        if s == 0:
            y[0:ch, here] = total[:, : max(ch, min(128, total.shape[1]))].T[0:ch]
            after[0](n)
        if s == planes - 1:
            y[ch:, here] = total.T[ch:]
            after[1](n)
        return carry

    lax.fori_loop(0, cells // chunk, step, 0)


def finish(y, rim, out, n):
    planes, ch, _ = out.shape
    here = slice(n * CHUNK, (n + 1) * CHUNK)
    for d in range(planes):
        total = y[(d + 1) * ch : (d + 2) * ch, here]
        if d == 0:
            total = total + rim[0, :, here]
        if d == planes - 1:
            total = total + rim[1, :, here]
        out[d, :, here] = total.astype(out.dtype)


def moved(v, by):
    if by == 0:
        return v
    return jnp.concatenate([v[:, v.shape[1] - by :], v[:, : v.shape[1] - by]], axis=1)


def group_of(S):
    return next(n for n in (8, 4, 2, 1) if S % n == 0)


def kernel(
    S, C, factor,
    x, g, w,
    feat, igrad, dw,
    xg, gg, wf, we, wg, xt, gt, px, pg, yx, yg, g3, grim, xrim, irim, dwa, dwt, dwp, dwq, dwr,
    own_sem, xu_s, xu_r, xd_s, xd_r, gu_s, gu_r, gd_s, gd_r,
    w_s, w_r, v_s, v_r, a_s, a_r, gr_s, gr_r, xr_s, xr_r, ir_s, ir_r, d_s, d_r,
):
    planes, ch, cells = x.shape
    cs = dw.shape[1]
    me_s = lax.axis_index("slab")
    me_c = lax.axis_index("chan")
    group = group_of(S)
    many = 8 // group
    base = lax.div(me_s, group) * group
    place = me_s - base

    barrier = pltpu.get_barrier_semaphore()
    for k in range(1, S):
        pl.semaphore_signal(barrier, inc=1, device_id={"slab": lax.rem(me_s + k, S)}, device_id_type=MESH)
    for k in range(1, C):
        pl.semaphore_signal(barrier, inc=1, device_id={"chan": lax.rem(me_c + k, C)}, device_id_type=MESH)
    pl.semaphore_wait(barrier, S - 1 + C - 1)

    def rows_of(j):
        return pl.ds(pl.multiple_of(j * ch, ch), ch)

    def to_chan(peer, src, dst, send, recv):
        return pltpu.make_async_remote_copy(
            src_ref=src, dst_ref=dst, send_sem=send, recv_sem=recv,
            device_id={"chan": peer}, device_id_type=MESH,
        )

    def to_slab(peer, src, dst, send, recv):
        return pltpu.make_async_remote_copy(
            src_ref=src, dst_ref=dst, send_sem=send, recv_sem=recv,
            device_id={"slab": peer}, device_id_type=MESH,
        )

    right, left = lax.rem(me_s + 1, S), lax.rem(me_s + S - 1, S)

    class Unit:
        def __init__(self, src, dst, s, us, ur, ds, dr):
            self.src, self.dst, self.s = src, dst, s
            self.sems = ((1, us, ur), (-1, ds, dr))

        def copy(self, way, send, recv, h, origin):
            rows = rows_of(lax.rem(me_c - way * origin + C, C))
            dst = self.dst.at[self.s, rows, :]
            src = self.src.at[self.s] if origin == 0 else dst
            peer = lax.rem(me_c + way * (h - origin) + C, C)
            return to_chan(peer, src, dst, send.at[self.s, h - 1], recv.at[self.s, h - 1])

        def sends(self, act, origin):
            for h in (origin + 2, origin + 1):
                if h > C - 1:
                    continue
                for way, send, recv in self.sems:
                    first, last = me_c - way * origin, me_c + way * (h - origin)
                    ok = (first >= 0) & (first <= C - 1) & (last >= 0) & (last <= C - 1)
                    pl.when(ok)(lambda c=self.copy(way, send, recv, h, origin): act(c))

        def take(self, h):
            for way, send, recv in self.sems:
                first = me_c - way * h
                pl.when((first >= 0) & (first <= C - 1))(
                    lambda c=self.copy(way, send, recv, h, h): c.wait_recv()
                )

        def start(self):
            self.sends(lambda c: c.start(), 0)

        def relay(self):
            for h in range(2, C - 1, 2):
                self.take(h)
                self.sends(lambda c: c.start(), h)

        def rest(self):
            for h in range(1, C):
                if h % 2 == 1 or h >= C - 1:
                    self.take(h)

        def drain(self):
            for origin in range(0, C - 1, 2):
                self.sends(lambda c: c.wait_send(), origin)

    xu = [Unit(x, xg, s, xu_s, xu_r, xd_s, xd_r) for s in range(planes)]
    gu = [Unit(g, gg, s, gu_s, gu_r, gd_s, gd_r) for s in range(planes)]
    units = xu + gu
    mine = rows_of(me_c)

    units[0].start()
    g_rims = [
        to_slab(left, g.at[0], grim.at[1], gr_s.at[1], gr_r.at[1]),
        to_slab(right, g.at[planes - 1], grim.at[0], gr_s.at[0], gr_r.at[0]),
    ]
    for c in g_rims:
        c.start()
    own = [
        pltpu.make_async_copy(x, xg.at[:, mine, :], own_sem.at[0]),
        pltpu.make_async_copy(g, gg.at[:, mine, :], own_sem.at[1]),
    ]
    for c in own:
        c.start()

    blank = [jnp.zeros((ch, (planes - 1) * ch), F32)] if planes > 1 else []

    def split_weights(t, carry):
        taps = [w[9 * p + t].astype(F32) for p in range(3)]
        for z in range(C):
            parts = [tap[:, z * ch : (z + 1) * ch] for tap in taps] + blank
            we[z, 8 - t] = jnp.concatenate(parts, axis=1).astype(BF16)
        return carry

    lax.fori_loop(0, 9, split_weights, 0)
    block = pl.ds(place * many, many)
    w_copies = []
    for k in range(1, C):
        peer = lax.rem(me_c + k, C)
        w_copies += [
            to_chan(peer, we.at[peer, block], wg.at[0, block, mine, :], w_s.at[k - 1], w_r.at[k - 1]),
            to_chan(peer, we.at[peer, 8], wg.at[0, 8, mine, :], v_s.at[k - 1], v_r.at[k - 1]),
        ]
    for c in w_copies:
        c.start()
    own += [
        pltpu.make_async_copy(we.at[me_c, block], wg.at[0, block, mine, :], own_sem.at[2]),
        pltpu.make_async_copy(we.at[me_c, 8], wg.at[0, 8, mine, :], own_sem.at[3]),
    ]
    for c in own[2:]:
        c.start()

    def turn_weights(t, carry):
        blocks = [w[9 * p + t].astype(F32) for p in (2, 1, 0)]
        if planes > 1:
            blocks.append(jnp.zeros(((planes - 1) * ch, C * ch), F32))
        turned = jnp.concatenate(blocks, axis=0).T
        for s in range(planes):
            wf[s, t] = moved(turned, s * ch).astype(BF16)
        return carry

    lax.fori_loop(0, 9, turn_weights, 0)
    units[0].relay()
    units[1].start()
    for c in own:
        c.wait()
    for c in g_rims:
        c.wait()
    for s in range(planes):
        for p in range(3):
            d = s - (p - 1)
            plane = grim[0] if d < 0 else grim[1] if d >= planes else g[d]
            g3[s, p * ch : (p + 1) * ch, :] = plane
    a_copies = [
        to_slab(
            base + lax.rem(place + k, group),
            wg.at[0, block], wg.at[0, block], a_s.at[k - 1], a_r.at[k - 1],
        )
        for k in range(1, group)
    ]
    for c in w_copies:
        c.wait()
    for c in a_copies:
        c.start()

    def weight_step(s, t, carry):
        total = jnp.dot(
            g3[s],
            xt[lax.rem(t, 3), s, pl.ds(pl.multiple_of(lax.div(t, 3) * W, W), cells), :],
            preferred_element_type=F32,
        )
        if s > 0:
            total = total + dwa[t]
        if s < planes - 1:
            dwa[t] = total
        else:
            turned = total.T
            for k in range(S):
                dwt[k % 2, k // 2, t] = turned[k * cs : (k + 1) * cs]
        return carry

    def x_rim(n):
        return rim_copies(yx, xrim, xr_s, xr_r, n)

    def i_rim(n):
        return rim_copies(yg, irim, ir_s, ir_r, n)

    def rim_copies(y, rim, send, recv, n):
        here = pl.ds(n * CHUNK if isinstance(n, int) else pl.multiple_of(n * CHUNK, CHUNK), CHUNK)
        return (
            lambda: to_slab(left, y.at[0:ch, here], rim.at[1, :, here], send.at[1, n], recv.at[1, n]),
            lambda: to_slab(
                right, y.at[(planes + 1) * ch : (planes + 2) * ch, here], rim.at[0, :, here],
                send.at[0, n], recv.at[0, n],
            ),
        )

    def starts(rim):
        return (lambda n: rim(n)[0]().start()), (lambda n: rim(n)[1]().start())

    def start_all(copies):
        for c in copies:
            c.start()

    even = lax.rem(me_s, 2)
    pair = lax.div(me_s, 2)
    pairs = S // 2
    p_copy = to_slab(me_s + 1 - 2 * even, dwt.at[1 - even], dwp, own_sem.at[4], own_sem.at[5])
    d_copies = []
    for k in range(1, pairs):
        other = lax.rem(pair + k, pairs)
        d_copies.append(
            to_slab(2 * other + even, dwq.at[other], dwr.at[k - 1], d_s.at[k - 1], d_r.at[k - 1])
        )

    def place_weights(t, carry):
        v = wg[0, t].astype(F32)
        for s in range(1, planes):
            wg[s, t] = moved(v, s * ch).astype(BF16)
        return carry

    def relay(i):
        if i < len(units):
            units[i].relay()

    def rest(i):
        units[i].rest()
        if i + 2 < len(units):
            units[i + 2].start()

    for s in range(planes):
        rest(s)
        turn_and_shift(xg, xt, s)
        lax.fori_loop(0, 9, functools.partial(weight_step, s), 0)
        if s == planes - 1:
            p_copy.start()
        relay(s + 1)
        conv(xt, wf, px, yx, s, starts(x_rim))
        if s == planes - 1:
            p_copy.wait()
            for m in range(pairs):
                dwq[m] = dwt[even, m] + dwp[m]
            start_all(d_copies)
        if s == 0:
            for c in a_copies:
                c.wait()
            lax.fori_loop(0, 9, place_weights, 0)
    chunks = cells // CHUNK
    for s in range(planes):
        rest(planes + s)
        turn_and_shift(gg, gt, s)
        relay(planes + s + 1)
        conv(gt, wg, pg, yg, s, starts(i_rim))
        if s == 0:
            for n in range(chunks):
                for c in x_rim(n):
                    c().wait()
                finish(yx, xrim, feat, n)
            for c in d_copies:
                c.wait()
            total = dwq[pair]
            for k in range(pairs - 1):
                total = total + dwr[k]
            total = total * factor
            for p in range(3):
                dw[9 * p : 9 * p + 9] = total[:, :, p * ch : (p + 1) * ch]
    for u in units:
        u.drain()
    for n in range(chunks):
        for c in i_rim(n):
            c().wait()
        finish(yg, irim, igrad, n)


def local(inputs, filters, cotangent):
    S = lax.axis_size("slab")
    C = lax.axis_size("chan")
    ch, planes, cells = inputs.shape
    wide = C * ch
    cs = wide // S
    group = group_of(S)
    spread = (planes + 2) * ch
    factor = 1.0 / math.sqrt(planes * S * cells)
    x = inputs.transpose(1, 0, 2)
    g = cotangent.transpose(1, 0, 2)
    dma = pltpu.SemaphoreType.DMA
    vmem = pl.BlockSpec(memory_space=pltpu.VMEM)
    feat, igrad, dw = pl.pallas_call(
        functools.partial(kernel, S, C, factor),
        out_shape=(
            jax.ShapeDtypeStruct((planes, ch, cells), BF16),
            jax.ShapeDtypeStruct((planes, ch, cells), BF16),
            jax.ShapeDtypeStruct((27, cs, ch), F32),
        ),
        in_specs=[vmem] * 3,
        out_specs=[vmem] * 3,
        scratch_shapes=[
            pltpu.VMEM((planes, wide, cells), BF16),
            pltpu.VMEM((planes, wide, cells), BF16),
            pltpu.VMEM((planes, 9, wide, spread), BF16),
            pltpu.VMEM((C, 9, ch, spread), BF16),
            pltpu.VMEM((planes, 9, wide, spread), BF16),
            pltpu.VMEM((3, planes, cells + 2 * W, wide), BF16),
            pltpu.VMEM((3, planes, cells + 2 * W, wide), BF16),
            pltpu.VMEM((cells, spread), F32),
            pltpu.VMEM((cells, spread), F32),
            pltpu.VMEM((spread, cells), F32),
            pltpu.VMEM((spread, cells), F32),
            pltpu.VMEM((planes, 3 * ch, cells), BF16),
            pltpu.VMEM((2, ch, cells), BF16),
            pltpu.VMEM((2, ch, cells), F32),
            pltpu.VMEM((2, ch, cells), F32),
            pltpu.VMEM((9, 3 * ch, wide), F32),
            pltpu.VMEM((2, S // 2, 9, cs, 3 * ch), F32),
            pltpu.VMEM((S // 2, 9, cs, 3 * ch), F32),
            pltpu.VMEM((S // 2, 9, cs, 3 * ch), F32),
            pltpu.VMEM((S // 2 - 1, 9, cs, 3 * ch), F32),
            dma((6,)),
        ]
        + [dma((planes, C - 1))] * 8
        + [dma((C - 1,))] * 4
        + [dma((max(group - 1, 1),))] * 2
        + [dma((2,))] * 2
        + [dma((2, cells // CHUNK))] * 4
        + [dma((S // 2 - 1,))] * 2,
        compiler_params=pltpu.CompilerParams(
            collective_id=0, has_side_effects=True, vmem_limit_bytes=48 * 1024 * 1024
        ),
    )(x, g, filters)
    return (feat.transpose(1, 0, 2), igrad.transpose(1, 0, 2), dw.transpose(0, 2, 1))


def solution(mesh):
    placed = (P("chan", "slab", None), P(None, "chan", None), P("chan", "slab", None))
    return jax.shard_map(
        local,
        mesh=mesh,
        in_specs=placed,
        out_specs=(P("chan", "slab", None), P("chan", "slab", None), P(None, "chan", "slab")),
        check_vma=False,
    )
```

```python
import functools
import math

import jax
import jax.numpy as jnp
from jax import lax
from jax.experimental import pallas as pl
from jax.experimental.pallas import tpu as pltpu
from jax.sharding import PartitionSpec as P

W = 64
CHUNK = 512
MESH = pl.DeviceIdType.MESH
F32 = jnp.float32
BF16 = jnp.bfloat16


def turn_and_shift(src, dst, s):
    cells = src.shape[2]

    def step(m, carry):
        turned = src[s, :, pl.ds(pl.multiple_of(m * 128, 128), 128)].T.astype(F32)
        for h in range(128 // W):
            row = turned[h * W : (h + 1) * W]
            at = pl.ds(pl.multiple_of(m * 128 + (h + 1) * W, W), W)
            dst[0, s, at, :] = pltpu.roll(row, 1, 0).astype(BF16)
            dst[1, s, at, :] = row.astype(BF16)
            dst[2, s, at, :] = pltpu.roll(row, W - 1, 0).astype(BF16)
        return carry

    lax.fori_loop(0, cells // 128, step, 0, unroll=6)
    for r in range(3):
        dst[r, s, 0:W, :] = dst[r, s, cells : cells + W, :]
        dst[r, s, cells + W : cells + 2 * W, :] = dst[r, s, W : 2 * W, :]


def conv(src, weights, partial, y, s, after):
    planes = weights.shape[0]
    cells, spread = partial.shape
    ch = spread // (planes + 2)
    chunk = CHUNK

    def step(n, carry):
        here = pl.ds(pl.multiple_of(n * chunk, chunk), chunk)
        total = None if s == 0 else partial[here, :]
        for q in range(3):
            for r in range(3):
                part = jnp.dot(
                    src[r, s, pl.ds(pl.multiple_of(n * chunk + q * W, W), chunk), :],
                    weights[s, 3 * q + r],
                    preferred_element_type=F32,
                )
                total = part if total is None else total + part
        if s < planes - 1:
            partial[here, :] = total
        if s == 0:
            y[0:ch, here] = total[:, : max(ch, min(128, total.shape[1]))].T[0:ch]
            after[0](n)
        if s == planes - 1:
            y[ch:, here] = total.T[ch:]
            after[1](n)
        return carry

    lax.fori_loop(0, cells // chunk, step, 0, unroll=True)


def finish(y, rim, out, n):
    planes, ch, _ = out.shape
    here = slice(n * CHUNK, (n + 1) * CHUNK)
    for d in range(planes):
        total = y[(d + 1) * ch : (d + 2) * ch, here]
        if d == 0:
            total = total + rim[0, :, here]
        if d == planes - 1:
            total = total + rim[1, :, here]
        out[d, :, here] = total.astype(out.dtype)


def moved(v, by):
    if by == 0:
        return v
    return jnp.concatenate([v[:, v.shape[1] - by :], v[:, : v.shape[1] - by]], axis=1)


def group_of(S):
    return next(n for n in (8, 4, 2, 1) if S % n == 0)


def kernel(
    S, C, factor,
    x, g, w,
    feat, igrad, dw,
    xg, gg, wf, we, wg, xt, gt, px, pg, yx, yg, g3, grim, xrim, irim, dwa, dwt, dwp, dwq, dwr,
    own_sem, xu_s, xu_r, xd_s, xd_r, gu_s, gu_r, gd_s, gd_r,
    w_s, w_r, v_s, v_r, a_s, a_r, gr_s, gr_r, xr_s, xr_r, ir_s, ir_r, d_s, d_r,
):
    planes, ch, cells = x.shape
    cs = dw.shape[1]
    me_s = lax.axis_index("slab")
    me_c = lax.axis_index("chan")
    group = group_of(S)
    many = 8 // group
    base = lax.div(me_s, group) * group
    place = me_s - base

    barrier = pltpu.get_barrier_semaphore()
    for k in range(1, S):
        pl.semaphore_signal(barrier, inc=1, device_id={"slab": lax.rem(me_s + k, S)}, device_id_type=MESH)
    for k in range(1, C):
        pl.semaphore_signal(barrier, inc=1, device_id={"chan": lax.rem(me_c + k, C)}, device_id_type=MESH)
    pl.semaphore_wait(barrier, S - 1 + C - 1)

    def rows_of(j):
        return pl.ds(pl.multiple_of(j * ch, ch), ch)

    def to_chan(peer, src, dst, send, recv):
        return pltpu.make_async_remote_copy(
            src_ref=src, dst_ref=dst, send_sem=send, recv_sem=recv,
            device_id={"chan": peer}, device_id_type=MESH,
        )

    def to_slab(peer, src, dst, send, recv):
        return pltpu.make_async_remote_copy(
            src_ref=src, dst_ref=dst, send_sem=send, recv_sem=recv,
            device_id={"slab": peer}, device_id_type=MESH,
        )

    right, left = lax.rem(me_s + 1, S), lax.rem(me_s + S - 1, S)

    class Unit:
        def __init__(self, src, dst, s, us, ur, ds, dr):
            self.src, self.dst, self.s = src, dst, s
            self.sems = ((1, us, ur), (-1, ds, dr))

        def copy(self, way, send, recv, h, origin):
            rows = rows_of(lax.rem(me_c - way * origin + C, C))
            dst = self.dst.at[self.s, rows, :]
            src = self.src.at[self.s] if origin == 0 else dst
            peer = lax.rem(me_c + way * (h - origin) + C, C)
            return to_chan(peer, src, dst, send.at[self.s, h - 1], recv.at[self.s, h - 1])

        def sends(self, act, origin):
            for h in (origin + 2, origin + 1):
                if h > C - 1:
                    continue
                for way, send, recv in self.sems:
                    first, last = me_c - way * origin, me_c + way * (h - origin)
                    ok = (first >= 0) & (first <= C - 1) & (last >= 0) & (last <= C - 1)
                    pl.when(ok)(lambda c=self.copy(way, send, recv, h, origin): act(c))

        def take(self, h):
            for way, send, recv in self.sems:
                first = me_c - way * h
                pl.when((first >= 0) & (first <= C - 1))(
                    lambda c=self.copy(way, send, recv, h, h): c.wait_recv()
                )

        def start(self):
            self.sends(lambda c: c.start(), 0)

        def relay(self):
            for h in range(2, C - 1, 2):
                self.take(h)
                self.sends(lambda c: c.start(), h)

        def rest(self):
            for h in range(1, C):
                if h % 2 == 1 or h >= C - 1:
                    self.take(h)

        def drain(self):
            for origin in range(0, C - 1, 2):
                self.sends(lambda c: c.wait_send(), origin)

    xu = [Unit(x, xg, s, xu_s, xu_r, xd_s, xd_r) for s in range(planes)]
    gu = [Unit(g, gg, s, gu_s, gu_r, gd_s, gd_r) for s in range(planes)]
    units = xu + gu
    mine = rows_of(me_c)

    units[0].start()
    g_rims = [
        to_slab(left, g.at[0], grim.at[1], gr_s.at[1], gr_r.at[1]),
        to_slab(right, g.at[planes - 1], grim.at[0], gr_s.at[0], gr_r.at[0]),
    ]
    for c in g_rims:
        c.start()
    own = [
        pltpu.make_async_copy(x, xg.at[:, mine, :], own_sem.at[0]),
        pltpu.make_async_copy(g, gg.at[:, mine, :], own_sem.at[1]),
    ]
    for c in own:
        c.start()

    blank = [jnp.zeros((ch, (planes - 1) * ch), F32)] if planes > 1 else []

    def split_weights(t, carry):
        taps = [w[9 * p + t].astype(F32) for p in range(3)]
        for z in range(C):
            parts = [tap[:, z * ch : (z + 1) * ch] for tap in taps] + blank
            we[z, 8 - t] = jnp.concatenate(parts, axis=1).astype(BF16)
        return carry

    lax.fori_loop(0, 9, split_weights, 0, unroll=3)
    block = pl.ds(place * many, many)
    w_copies = []
    for k in range(1, C):
        peer = lax.rem(me_c + k, C)
        w_copies += [
            to_chan(peer, we.at[peer, block], wg.at[0, block, mine, :], w_s.at[k - 1], w_r.at[k - 1]),
            to_chan(peer, we.at[peer, 8], wg.at[0, 8, mine, :], v_s.at[k - 1], v_r.at[k - 1]),
        ]
    for c in w_copies:
        c.start()
    own += [
        pltpu.make_async_copy(we.at[me_c, block], wg.at[0, block, mine, :], own_sem.at[2]),
        pltpu.make_async_copy(we.at[me_c, 8], wg.at[0, 8, mine, :], own_sem.at[3]),
    ]
    for c in own[2:]:
        c.start()

    def turn_weights(t, carry):
        blocks = [w[9 * p + t].astype(F32) for p in (2, 1, 0)]
        if planes > 1:
            blocks.append(jnp.zeros(((planes - 1) * ch, C * ch), F32))
        turned = jnp.concatenate(blocks, axis=0).T
        for s in range(planes):
            wf[s, t] = moved(turned, s * ch).astype(BF16)
        return carry

    lax.fori_loop(0, 9, turn_weights, 0, unroll=3)
    units[0].relay()
    units[1].start()
    for c in own:
        c.wait()
    for c in g_rims:
        c.wait()
    for s in range(planes):
        for p in range(3):
            d = s - (p - 1)
            plane = grim[0] if d < 0 else grim[1] if d >= planes else g[d]
            g3[s, p * ch : (p + 1) * ch, :] = plane
    a_copies = [
        to_slab(
            base + lax.rem(place + k, group),
            wg.at[0, block], wg.at[0, block], a_s.at[k - 1], a_r.at[k - 1],
        )
        for k in range(1, group)
    ]
    for c in w_copies:
        c.wait()
    for c in a_copies:
        c.start()

    def weight_step(s, t, carry):
        total = jnp.dot(
            g3[s],
            xt[lax.rem(t, 3), s, pl.ds(pl.multiple_of(lax.div(t, 3) * W, W), cells), :],
            preferred_element_type=F32,
        )
        if s > 0:
            total = total + dwa[t]
        if s < planes - 1:
            dwa[t] = total
        else:
            turned = total.T
            for k in range(S):
                dwt[k % 2, k // 2, t] = turned[k * cs : (k + 1) * cs]
        return carry

    def x_rim(n):
        return rim_copies(yx, xrim, xr_s, xr_r, n)

    def i_rim(n):
        return rim_copies(yg, irim, ir_s, ir_r, n)

    def rim_copies(y, rim, send, recv, n):
        here = pl.ds(n * CHUNK if isinstance(n, int) else pl.multiple_of(n * CHUNK, CHUNK), CHUNK)
        return (
            lambda: to_slab(left, y.at[0:ch, here], rim.at[1, :, here], send.at[1, n], recv.at[1, n]),
            lambda: to_slab(
                right, y.at[(planes + 1) * ch : (planes + 2) * ch, here], rim.at[0, :, here],
                send.at[0, n], recv.at[0, n],
            ),
        )

    def starts(rim):
        return (lambda n: rim(n)[0]().start()), (lambda n: rim(n)[1]().start())

    def start_all(copies):
        for c in copies:
            c.start()

    even = lax.rem(me_s, 2)
    pair = lax.div(me_s, 2)
    pairs = S // 2
    p_copy = to_slab(me_s + 1 - 2 * even, dwt.at[1 - even], dwp, own_sem.at[4], own_sem.at[5])
    d_copies = []
    for k in range(1, pairs):
        other = lax.rem(pair + k, pairs)
        d_copies.append(
            to_slab(2 * other + even, dwq.at[other], dwr.at[k - 1], d_s.at[k - 1], d_r.at[k - 1])
        )

    def place_weights(t, carry):
        v = wg[0, t].astype(F32)
        for s in range(1, planes):
            wg[s, t] = moved(v, s * ch).astype(BF16)
        return carry

    def relay(i):
        if i < len(units):
            units[i].relay()

    def rest(i):
        units[i].rest()
        if i + 2 < len(units):
            units[i + 2].start()

    for s in range(planes):
        rest(s)
        turn_and_shift(xg, xt, s)
        lax.fori_loop(0, 9, functools.partial(weight_step, s), 0, unroll=3)
        if s == planes - 1:
            p_copy.start()
        relay(s + 1)
        conv(xt, wf, px, yx, s, starts(x_rim))
        if s == planes - 1:
            p_copy.wait()
            for m in range(pairs):
                dwq[m] = dwt[even, m] + dwp[m]
            start_all(d_copies)
        if s == 0:
            for c in a_copies:
                c.wait()
            lax.fori_loop(0, 9, place_weights, 0, unroll=3)
    chunks = cells // CHUNK
    for s in range(planes):
        rest(planes + s)
        turn_and_shift(gg, gt, s)
        relay(planes + s + 1)
        conv(gt, wg, pg, yg, s, starts(i_rim))
        if s == 0:
            for n in range(chunks):
                for c in x_rim(n):
                    c().wait()
                finish(yx, xrim, feat, n)
            for c in d_copies:
                c.wait()
            total = dwq[pair]
            for k in range(pairs - 1):
                total = total + dwr[k]
            total = total * factor
            for p in range(3):
                dw[9 * p : 9 * p + 9] = total[:, :, p * ch : (p + 1) * ch]
    for u in units:
        u.drain()
    for n in range(chunks):
        for c in i_rim(n):
            c().wait()
        finish(yg, irim, igrad, n)


def local(inputs, filters, cotangent):
    S = lax.axis_size("slab")
    C = lax.axis_size("chan")
    ch, planes, cells = inputs.shape
    wide = C * ch
    cs = wide // S
    group = group_of(S)
    spread = (planes + 2) * ch
    factor = 1.0 / math.sqrt(planes * S * cells)
    x = inputs.transpose(1, 0, 2)
    g = cotangent.transpose(1, 0, 2)
    dma = pltpu.SemaphoreType.DMA
    vmem = pl.BlockSpec(memory_space=pltpu.VMEM)
    feat, igrad, dw = pl.pallas_call(
        functools.partial(kernel, S, C, factor),
        out_shape=(
            jax.ShapeDtypeStruct((planes, ch, cells), BF16),
            jax.ShapeDtypeStruct((planes, ch, cells), BF16),
            jax.ShapeDtypeStruct((27, cs, ch), F32),
        ),
        in_specs=[vmem] * 3,
        out_specs=[vmem] * 3,
        scratch_shapes=[
            pltpu.VMEM((planes, wide, cells), BF16),
            pltpu.VMEM((planes, wide, cells), BF16),
            pltpu.VMEM((planes, 9, wide, spread), BF16),
            pltpu.VMEM((C, 9, ch, spread), BF16),
            pltpu.VMEM((planes, 9, wide, spread), BF16),
            pltpu.VMEM((3, planes, cells + 2 * W, wide), BF16),
            pltpu.VMEM((3, planes, cells + 2 * W, wide), BF16),
            pltpu.VMEM((cells, spread), F32),
            pltpu.VMEM((cells, spread), F32),
            pltpu.VMEM((spread, cells), F32),
            pltpu.VMEM((spread, cells), F32),
            pltpu.VMEM((planes, 3 * ch, cells), BF16),
            pltpu.VMEM((2, ch, cells), BF16),
            pltpu.VMEM((2, ch, cells), F32),
            pltpu.VMEM((2, ch, cells), F32),
            pltpu.VMEM((9, 3 * ch, wide), F32),
            pltpu.VMEM((2, S // 2, 9, cs, 3 * ch), F32),
            pltpu.VMEM((S // 2, 9, cs, 3 * ch), F32),
            pltpu.VMEM((S // 2, 9, cs, 3 * ch), F32),
            pltpu.VMEM((S // 2 - 1, 9, cs, 3 * ch), F32),
            dma((6,)),
        ]
        + [dma((planes, C - 1))] * 8
        + [dma((C - 1,))] * 4
        + [dma((max(group - 1, 1),))] * 2
        + [dma((2,))] * 2
        + [dma((2, cells // CHUNK))] * 4
        + [dma((S // 2 - 1,))] * 2,
        compiler_params=pltpu.CompilerParams(
            collective_id=0, has_side_effects=True, vmem_limit_bytes=48 * 1024 * 1024
        ),
    )(x, g, filters)
    return (feat.transpose(1, 0, 2), igrad.transpose(1, 0, 2), dw.transpose(0, 2, 1))


def solution(mesh):
    placed = (P("chan", "slab", None), P(None, "chan", None), P("chan", "slab", None))
    return jax.shard_map(
        local,
        mesh=mesh,
        in_specs=placed,
        out_specs=(P("chan", "slab", None), P("chan", "slab", None), P(None, "chan", "slab")),
        check_vma=False,
    )
```

```python
import functools
import math

import jax
import jax.numpy as jnp
from jax import lax
from jax.experimental import pallas as pl
from jax.experimental.pallas import tpu as pltpu
from jax.sharding import PartitionSpec as P

W = 64
CHUNK = 512
MESH = pl.DeviceIdType.MESH
F32 = jnp.float32
BF16 = jnp.bfloat16


def turn_and_shift(src, dst, s):
    cells = src.shape[2]

    def step(m, carry):
        turned = src[s, :, pl.ds(pl.multiple_of(m * 128, 128), 128)].T.astype(F32)
        for h in range(128 // W):
            row = turned[h * W : (h + 1) * W]
            at = pl.ds(pl.multiple_of(m * 128 + (h + 1) * W, W), W)
            dst[0, s, at, :] = pltpu.roll(row, 1, 0).astype(BF16)
            dst[1, s, at, :] = row.astype(BF16)
            dst[2, s, at, :] = pltpu.roll(row, W - 1, 0).astype(BF16)
        return carry

    lax.fori_loop(0, cells // 128, step, 0, unroll=6)
    for r in range(3):
        dst[r, s, 0:W, :] = dst[r, s, cells : cells + W, :]
        dst[r, s, cells + W : cells + 2 * W, :] = dst[r, s, W : 2 * W, :]


def conv(src, weights, partial, y, s, after):
    planes = weights.shape[0]
    cells, spread = partial.shape
    ch = spread // (planes + 2)
    chunk = CHUNK

    def step(n, carry):
        here = pl.ds(pl.multiple_of(n * chunk, chunk), chunk)
        total = None if s == 0 else partial[here, :]
        for q in range(3):
            for r in range(3):
                part = jnp.dot(
                    src[r, s, pl.ds(pl.multiple_of(n * chunk + q * W, W), chunk), :],
                    weights[s, 3 * q + r],
                    preferred_element_type=F32,
                )
                total = part if total is None else total + part
        if s < planes - 1:
            partial[here, :] = total
        if s == 0:
            y[0:ch, here] = total[:, : max(ch, min(128, total.shape[1]))].T[0:ch]
            after[0](n)
        if s == planes - 1:
            y[ch:, here] = total.T[ch:]
            after[1](n)
        return carry

    lax.fori_loop(0, cells // chunk, step, 0, unroll=True)


def finish(y, rim, out, n):
    planes, ch, _ = out.shape
    here = slice(n * CHUNK, (n + 1) * CHUNK)
    for d in range(planes):
        total = y[(d + 1) * ch : (d + 2) * ch, here]
        if d == 0:
            total = total + rim[0, :, here]
        if d == planes - 1:
            total = total + rim[1, :, here]
        out[d, :, here] = total.astype(out.dtype)


def moved(v, by):
    if by == 0:
        return v
    return jnp.concatenate([v[:, v.shape[1] - by :], v[:, : v.shape[1] - by]], axis=1)


def group_of(S):
    return next(n for n in (8, 4, 2, 1) if S % n == 0)


def kernel(
    S, C, factor,
    x, g, w,
    feat, igrad, dw,
    xg, gg, wf, we, wg, xt, gt, px, pg, yx, yg, g3, grim, xrim, irim, dwa, dwt, dwp, dwq, dwr,
    own_sem, xu_s, xu_r, xd_s, xd_r, gu_s, gu_r, gd_s, gd_r,
    w_s, w_r, v_s, v_r, a_s, a_r, gr_s, gr_r, xr_s, xr_r, ir_s, ir_r, d_s, d_r,
):
    planes, ch, cells = x.shape
    cs = dw.shape[1]
    me_s = lax.axis_index("slab")
    me_c = lax.axis_index("chan")
    group = group_of(S)
    many = 8 // group
    base = lax.div(me_s, group) * group
    place = me_s - base

    barrier = pltpu.get_barrier_semaphore()
    for k in range(1, S):
        pl.semaphore_signal(barrier, inc=1, device_id={"slab": lax.rem(me_s + k, S)}, device_id_type=MESH)
    for k in range(1, C):
        pl.semaphore_signal(barrier, inc=1, device_id={"chan": lax.rem(me_c + k, C)}, device_id_type=MESH)
    pl.semaphore_wait(barrier, S - 1 + C - 1)

    def rows_of(j):
        return pl.ds(pl.multiple_of(j * ch, ch), ch)

    def to_chan(peer, src, dst, send, recv):
        return pltpu.make_async_remote_copy(
            src_ref=src, dst_ref=dst, send_sem=send, recv_sem=recv,
            device_id={"chan": peer}, device_id_type=MESH,
        )

    def to_slab(peer, src, dst, send, recv):
        return pltpu.make_async_remote_copy(
            src_ref=src, dst_ref=dst, send_sem=send, recv_sem=recv,
            device_id={"slab": peer}, device_id_type=MESH,
        )

    right, left = lax.rem(me_s + 1, S), lax.rem(me_s + S - 1, S)

    class Unit:
        def __init__(self, src, dst, s, us, ur, ds, dr):
            self.src, self.dst, self.s = src, dst, s
            self.sems = ((1, us, ur), (-1, ds, dr))

        def copy(self, way, send, recv, h, origin):
            rows = rows_of(lax.rem(me_c - way * origin + C, C))
            dst = self.dst.at[self.s, rows, :]
            src = self.src.at[self.s] if origin == 0 else dst
            peer = lax.rem(me_c + way * (h - origin) + C, C)
            return to_chan(peer, src, dst, send.at[self.s, h - 1], recv.at[self.s, h - 1])

        def sends(self, act, origin):
            for h in (origin + 2, origin + 1):
                if h > C - 1:
                    continue
                for way, send, recv in self.sems:
                    first, last = me_c - way * origin, me_c + way * (h - origin)
                    ok = (first >= 0) & (first <= C - 1) & (last >= 0) & (last <= C - 1)
                    pl.when(ok)(lambda c=self.copy(way, send, recv, h, origin): act(c))

        def take(self, h):
            for way, send, recv in self.sems:
                first = me_c - way * h
                pl.when((first >= 0) & (first <= C - 1))(
                    lambda c=self.copy(way, send, recv, h, h): c.wait_recv()
                )

        def start(self):
            self.sends(lambda c: c.start(), 0)

        def relay(self):
            for h in range(2, C - 1, 2):
                self.take(h)
                self.sends(lambda c: c.start(), h)

        def rest(self):
            for h in range(1, C):
                if h % 2 == 1 or h >= C - 1:
                    self.take(h)

        def drain(self):
            for origin in range(0, C - 1, 2):
                self.sends(lambda c: c.wait_send(), origin)

    xu = [Unit(x, xg, s, xu_s, xu_r, xd_s, xd_r) for s in range(planes)]
    gu = [Unit(g, gg, s, gu_s, gu_r, gd_s, gd_r) for s in range(planes)]
    units = xu + gu
    mine = rows_of(me_c)

    units[0].start()
    g_rims = [
        to_slab(left, g.at[0], grim.at[1], gr_s.at[1], gr_r.at[1]),
        to_slab(right, g.at[planes - 1], grim.at[0], gr_s.at[0], gr_r.at[0]),
    ]
    for c in g_rims:
        c.start()
    own = [
        pltpu.make_async_copy(x, xg.at[:, mine, :], own_sem.at[0]),
        pltpu.make_async_copy(g, gg.at[:, mine, :], own_sem.at[1]),
    ]
    for c in own:
        c.start()

    blank = [jnp.zeros((ch, (planes - 1) * ch), F32)] if planes > 1 else []

    def split_weights(t, carry):
        taps = [w[9 * p + t].astype(F32) for p in range(3)]
        for z in range(C):
            parts = [tap[:, z * ch : (z + 1) * ch] for tap in taps] + blank
            we[z, 8 - t] = jnp.concatenate(parts, axis=1).astype(BF16)
        return carry

    lax.fori_loop(0, 9, split_weights, 0, unroll=3)
    block = pl.ds(place * many, many)
    w_copies = []
    for k in range(1, C):
        peer = lax.rem(me_c + k, C)
        w_copies += [
            to_chan(peer, we.at[peer, block], wg.at[0, block, mine, :], w_s.at[k - 1], w_r.at[k - 1]),
            to_chan(peer, we.at[peer, 8], wg.at[0, 8, mine, :], v_s.at[k - 1], v_r.at[k - 1]),
        ]
    for c in w_copies:
        c.start()
    own += [
        pltpu.make_async_copy(we.at[me_c, block], wg.at[0, block, mine, :], own_sem.at[2]),
        pltpu.make_async_copy(we.at[me_c, 8], wg.at[0, 8, mine, :], own_sem.at[3]),
    ]
    for c in own[2:]:
        c.start()

    def turn_weights(t, carry):
        blocks = [w[9 * p + t].astype(F32) for p in (2, 1, 0)]
        if planes > 1:
            blocks.append(jnp.zeros(((planes - 1) * ch, C * ch), F32))
        turned = jnp.concatenate(blocks, axis=0).T
        for s in range(planes):
            wf[s, t] = moved(turned, s * ch).astype(BF16)
        return carry

    lax.fori_loop(0, 9, turn_weights, 0, unroll=3)
    units[0].relay()
    units[1].start()
    for c in own:
        c.wait()
    for c in g_rims:
        c.wait()
    for s in range(planes):
        for p in range(3):
            d = s - (p - 1)
            plane = grim[0] if d < 0 else grim[1] if d >= planes else g[d]
            g3[s, p * ch : (p + 1) * ch, :] = plane
    a_copies = [
        to_slab(
            base + lax.rem(place + k, group),
            wg.at[0, block], wg.at[0, block], a_s.at[k - 1], a_r.at[k - 1],
        )
        for k in range(1, group)
    ]
    for c in w_copies:
        c.wait()
    for c in a_copies:
        c.start()

    def weight_step(s, t, carry):
        total = jnp.dot(
            g3[s],
            xt[lax.rem(t, 3), s, pl.ds(pl.multiple_of(lax.div(t, 3) * W, W), cells), :],
            preferred_element_type=F32,
        )
        if s > 0:
            total = total + dwa[t]
        if s < planes - 1:
            dwa[t] = total
        else:
            turned = total.T
            for k in range(S):
                dwt[k % 2, k // 2, t] = turned[k * cs : (k + 1) * cs]
        return carry

    def x_rim(n):
        return rim_copies(yx, xrim, xr_s, xr_r, n)

    def i_rim(n):
        return rim_copies(yg, irim, ir_s, ir_r, n)

    def rim_copies(y, rim, send, recv, n):
        here = pl.ds(n * CHUNK if isinstance(n, int) else pl.multiple_of(n * CHUNK, CHUNK), CHUNK)
        return (
            lambda: to_slab(left, y.at[0:ch, here], rim.at[1, :, here], send.at[1, n], recv.at[1, n]),
            lambda: to_slab(
                right, y.at[(planes + 1) * ch : (planes + 2) * ch, here], rim.at[0, :, here],
                send.at[0, n], recv.at[0, n],
            ),
        )

    def starts(rim):
        return (lambda n: rim(n)[0]().start()), (lambda n: rim(n)[1]().start())

    def start_all(copies):
        for c in copies:
            c.start()

    even = lax.rem(me_s, 2)
    pair = lax.div(me_s, 2)
    pairs = S // 2
    p_copy = to_slab(me_s + 1 - 2 * even, dwt.at[1 - even], dwp, own_sem.at[4], own_sem.at[5])
    d_copies = []
    for k in range(1, pairs):
        other = lax.rem(pair + k, pairs)
        d_copies.append(
            to_slab(2 * other + even, dwq.at[other], dwr.at[k - 1], d_s.at[k - 1], d_r.at[k - 1])
        )

    def place_weights(t, carry):
        v = wg[0, t].astype(F32)
        for s in range(1, planes):
            wg[s, t] = moved(v, s * ch).astype(BF16)
        return carry

    def relay(i):
        if i < len(units):
            units[i].relay()

    def rest(i):
        units[i].rest()
        if i + 2 < len(units):
            units[i + 2].start()

    for s in range(planes):
        rest(s)
        turn_and_shift(xg, xt, s)
        lax.fori_loop(0, 9, functools.partial(weight_step, s), 0, unroll=3)
        if s == planes - 1:
            p_copy.start()
        relay(s + 1)
        if s == planes - 1:
            p_copy.wait()
            for m in range(pairs):
                dwq[m] = dwt[even, m] + dwp[m]
            start_all(d_copies)
        conv(xt, wf, px, yx, s, starts(x_rim))
        if s == 0:
            for c in a_copies:
                c.wait()
            lax.fori_loop(0, 9, place_weights, 0, unroll=3)
    chunks = cells // CHUNK
    for s in range(planes):
        rest(planes + s)
        turn_and_shift(gg, gt, s)
        relay(planes + s + 1)
        conv(gt, wg, pg, yg, s, starts(i_rim))
    for n in range(chunks):
        for c in x_rim(n):
            c().wait()
        finish(yx, xrim, feat, n)
    for c in d_copies:
        c.wait()
    total = dwq[pair]
    for k in range(pairs - 1):
        total = total + dwr[k]
    total = total * factor
    for p in range(3):
        dw[9 * p : 9 * p + 9] = total[:, :, p * ch : (p + 1) * ch]
    for u in units:
        u.drain()
    for n in range(chunks):
        for c in i_rim(n):
            c().wait()
        finish(yg, irim, igrad, n)


def local(inputs, filters, cotangent):
    S = lax.axis_size("slab")
    C = lax.axis_size("chan")
    ch, planes, cells = inputs.shape
    wide = C * ch
    cs = wide // S
    group = group_of(S)
    spread = (planes + 2) * ch
    factor = 1.0 / math.sqrt(planes * S * cells)
    x = inputs.transpose(1, 0, 2)
    g = cotangent.transpose(1, 0, 2)
    dma = pltpu.SemaphoreType.DMA
    vmem = pl.BlockSpec(memory_space=pltpu.VMEM)
    feat, igrad, dw = pl.pallas_call(
        functools.partial(kernel, S, C, factor),
        out_shape=(
            jax.ShapeDtypeStruct((planes, ch, cells), BF16),
            jax.ShapeDtypeStruct((planes, ch, cells), BF16),
            jax.ShapeDtypeStruct((27, cs, ch), F32),
        ),
        in_specs=[vmem] * 3,
        out_specs=[vmem] * 3,
        scratch_shapes=[
            pltpu.VMEM((planes, wide, cells), BF16),
            pltpu.VMEM((planes, wide, cells), BF16),
            pltpu.VMEM((planes, 9, wide, spread), BF16),
            pltpu.VMEM((C, 9, ch, spread), BF16),
            pltpu.VMEM((planes, 9, wide, spread), BF16),
            pltpu.VMEM((3, planes, cells + 2 * W, wide), BF16),
            pltpu.VMEM((3, planes, cells + 2 * W, wide), BF16),
            pltpu.VMEM((cells, spread), F32),
            pltpu.VMEM((cells, spread), F32),
            pltpu.VMEM((spread, cells), F32),
            pltpu.VMEM((spread, cells), F32),
            pltpu.VMEM((planes, 3 * ch, cells), BF16),
            pltpu.VMEM((2, ch, cells), BF16),
            pltpu.VMEM((2, ch, cells), F32),
            pltpu.VMEM((2, ch, cells), F32),
            pltpu.VMEM((9, 3 * ch, wide), F32),
            pltpu.VMEM((2, S // 2, 9, cs, 3 * ch), F32),
            pltpu.VMEM((S // 2, 9, cs, 3 * ch), F32),
            pltpu.VMEM((S // 2, 9, cs, 3 * ch), F32),
            pltpu.VMEM((S // 2 - 1, 9, cs, 3 * ch), F32),
            dma((6,)),
        ]
        + [dma((planes, C - 1))] * 8
        + [dma((C - 1,))] * 4
        + [dma((max(group - 1, 1),))] * 2
        + [dma((2,))] * 2
        + [dma((2, cells // CHUNK))] * 4
        + [dma((S // 2 - 1,))] * 2,
        compiler_params=pltpu.CompilerParams(
            collective_id=0, has_side_effects=True, vmem_limit_bytes=48 * 1024 * 1024
        ),
    )(x, g, filters)
    return (feat.transpose(1, 0, 2), igrad.transpose(1, 0, 2), dw.transpose(0, 2, 1))


def solution(mesh):
    placed = (P("chan", "slab", None), P(None, "chan", None), P("chan", "slab", None))
    return jax.shard_map(
        local,
        mesh=mesh,
        in_specs=placed,
        out_specs=(P("chan", "slab", None), P("chan", "slab", None), P(None, "chan", "slab")),
        check_vma=False,
    )
```
